128 devices in a mesh: expert: 32 (over x, y, core), shard: 4 (over z).
Axes of the slice: x: 4, y: 4, z: 4, core: 2. Of those that a mesh axis runs over, the one named last changes fastest.
Arguments:
- inputs: bfloat16 [16384, 1024], P(('expert', 'shard')), may hold values from -6 to 6
- route_ids: int32 [16384, 8], P(('expert', 'shard')), may hold values from 0 to 31, all different within a row; in each aligned block of 128 rows (0 to 127, 128 to 255, ...) at most 48 rows name the same one
- cotangent: bfloat16 [16384, 1024], P(('expert', 'shard')), may hold values from -6 to 6
- query_key_value_weight: float32 [1024, 2048], P(('expert', 'shard')), may hold values from -0.25 to 0.25
- projection_first_moment: float32 [1024, 2048], P(('expert', 'shard')), may hold values from -80 to 80
- projection_second_moment: float32 [1024, 2048], P(('expert', 'shard')), may hold values from 425.984 to 6881.28
- out_weight: float32 [1024, 1024], P(('expert', 'shard')), may hold values from -0.375 to 0.375
- out_moment_one: float32 [1024, 1024], P(('expert', 'shard')), may hold values from -48 to 48
- out_moment_two: float32 [1024, 1024], P(('expert', 'shard')), may hold values from 155.648 to 2457.6
- router_weight: float32 [1024, 32], P(('expert', 'shard')), may hold values from -0.09375 to 0.09375
- router_moment_one: float32 [1024, 32], P(('expert', 'shard')), may hold values from -384 to 384
- router_moment_two: float32 [1024, 32], P(('expert', 'shard')), may hold values from 9646.899 to 159383.55
- gain_weight: float32 [1024, 2], P(('expert', 'shard')), may hold values from 0.5 to 1.5
- gain_moment_one: float32 [1024, 2], P(('expert', 'shard')), may hold values from -160 to 160
- gain_moment_two: float32 [1024, 2], P(('expert', 'shard')), may hold values from 1638.4 to 27852.8
- expand_weight: float32 [32, 1024, 1024], P('expert', 'shard'), may hold values from -0.1875 to 0.1875
- expand_moment_one: float32 [32, 1024, 1024], P('expert', 'shard'), may hold values from -20 to 20
- expand_moment_two: float32 [32, 1024, 1024], P('expert', 'shard'), may hold values from 26.624 to 430.08
- reduce_weight: float32 [32, 512, 1024], P('expert', 'shard'), may hold values from -1 to 1
- reduce_moment_one: float32 [32, 512, 1024], P('expert', 'shard'), may hold values from -3 to 3
- reduce_moment_two: float32 [32, 512, 1024], P('expert', 'shard'), may hold values from 0.6144 to 9.8304
Outputs:
- outputs: bfloat16 [16384, 1024], P(('expert', 'shard'))
- input_grad: float32 [16384, 1024], P(('expert', 'shard'))
- qkv_one_new: float32 [1024, 2048], P(('expert', 'shard'))
- qkv_two_new: float32 [1024, 2048], P(('expert', 'shard'))
- qkv_new: float32 [1024, 2048], P(('expert', 'shard'))
- out_one_new: float32 [1024, 1024], P(('expert', 'shard'))
- out_two_new: float32 [1024, 1024], P(('expert', 'shard'))
- out_new: float32 [1024, 1024], P(('expert', 'shard'))
- router_one_new: float32 [1024, 32], P(('expert', 'shard'))
- router_two_new: float32 [1024, 32], P(('expert', 'shard'))
- router_new: float32 [1024, 32], P(('expert', 'shard'))
- gain_one_new: float32 [1024, 2], P(('expert', 'shard'))
- gain_two_new: float32 [1024, 2], P(('expert', 'shard'))
- gain_new: float32 [1024, 2], P(('expert', 'shard'))
- expand_one_new: float32 [32, 1024, 1024], P('expert', 'shard')
- expand_two_new: float32 [32, 1024, 1024], P('expert', 'shard')
- expand_new: float32 [32, 1024, 1024], P('expert', 'shard')
- reduce_one_new: float32 [32, 512, 1024], P('expert', 'shard')
- reduce_two_new: float32 [32, 512, 1024], P('expert', 'shard')
- reduce_new: float32 [32, 512, 1024], P('expert', 'shard')
The draws below stay inside these ranges and needn't reach their ends.
Inputs may be any that keep to these rules, and one draw needn't show every extreme that they name: `route_ids`: each row names 8 different experts. Among the 128 rows of one device no expert is named by more than 48 rows, and in every draw some expert is named by exactly 48 rows of some device.
All inputs are finite; a program needn't handle non-finite values.
Results may differ from the reference program's by a relative error of at most 0.023.
Values may be sent and summed in bfloat16 or wider, within the bound.
No kernel may reach another device: no remote copies, remote signals or barrier semaphores. Data moves between devices by JAX's collectives and lax.ppermute only.
A program may use at most 128 MiB of HBM per device.

```python
import math
from functools import partial
import jax
import jax.numpy as jnp
import numpy as np
from jax import lax

MODEL_DIMENSION = 1024
QUERY_HEAD_COUNT = 16
KEY_VALUE_HEADS = 8
HEAD_DIMENSION = 64
FF = 512
TOP = 8
STEP = 10
TOK_DEV = 128
EXPERTS = 32
SEQUENCE_TOKENS = 512
TOTAL_TOKENS = 16384
CAP = 48
N_EXPERT = 32
N_SHARD = 4


def steps_of(rng, shape, cuts, smallest, high):
    level, own = 1.0, jax.random.fold_in(rng, 6)
    for axis_at, blocks in cuts:
        steps = jnp.exp(jax.random.uniform(jax.random.fold_in(own, axis_at), (blocks,), jnp.float32, smallest / len(cuts), high / len(cuts)))
        level = level * jnp.repeat(steps, shape[axis_at] // blocks).reshape([-1 if axis == axis_at else 1 for axis in range(len(shape))])
    return level


def shared_out(own_key, own, number, rows, number_of, top, bound, skew):
    order = jax.random.permutation(own_key, number_of)
    packed, ordinary = shares(number_of, rows * top, bound, skew, True), shares(number_of, rows * top, bound, skew, False)
    places = jnp.arange(number_of)

    def named(sizes, turn):
        used = int((sizes > 0).sum())
        fixed = max(1, used // 4)
        passed = fixed + (places - fixed + turn * (used - fixed)) % max(1, number_of - fixed)
        return jnp.zeros((number_of,), jnp.int32).at[order[jnp.where(places < fixed, places, passed)]].set(jnp.asarray(sizes, jnp.int32))

    sizes = jnp.where(number % 4 == 0, named(packed, number // 4), named(ordinary, number - number // 4 - 1))
    mixed = jax.random.permutation(jax.random.fold_in(own, 3), number_of)
    giver, receiver = mixed[0:number_of // 2 * 2:2], mixed[1:number_of // 2 * 2:2]
    slack = jnp.minimum(sizes[giver] - 1, bound - sizes[receiver]) // 2
    slack = jnp.where((giver == order[0]) | (receiver == order[0]) | (sizes[receiver] == 0), 0, jnp.maximum(slack, 0))
    passed = jax.random.randint(jax.random.fold_in(own, 4), (number_of // 2,), 0, 1 << 20) % (slack + 1)
    sizes = sizes.at[giver].add(-passed).at[receiver].add(passed)
    labels = jnp.searchsorted(jnp.cumsum(sizes), jnp.arange(rows * top), side="right").astype(jnp.int32)
    listing = labels.reshape(top, rows).T
    listing = listing[jax.random.permutation(jax.random.fold_in(own, 1), rows)]
    turn = jax.random.randint(jax.random.fold_in(own, 2), (rows, 1), 0, top)
    return jnp.take_along_axis(listing, (jnp.arange(top)[None, :] + turn) % top, axis=1)


def shares(number_of, total, limit, slope, full):
    portions = [(1 << 20) // math.isqrt(standing ** slope) + 1 for standing in range(1, number_of + 1)]
    largest = limit if full else min(limit, max(-(-total // number_of), total * portions[0] // sum(portions)))
    least = 1 if total - largest >= number_of - 1 else 0
    counts, spare = [largest] + [least] * (number_of - 1), total - largest - least * (number_of - 1)
    while spare > 0:
        movable = [i for i in range(1, number_of) if counts[i] < largest] or [i for i in range(1, number_of) if counts[i] < limit]
        mass, budget = sum([portions[i] for i in movable]), spare
        for i in movable:
            extra = min(limit - counts[i], max(1, budget * portions[i] // mass), spare)
            counts[i] = counts[i] + extra
            spare = spare - extra
    return np.array(counts)


def normal_values(key, dims, spread, reach, shards=(), kind=jnp.bfloat16):
    values = jax.random.normal(key, dims, jnp.float32) * spread
    if len(shards) > 0:
        values = steps_of(key, dims, shards, -0.22, 0.18) * values
    return jnp.clip(values, min=-reach, max=reach).astype(kind)


def setup_inputs(seed: int = 0) -> dict:
    seeds = jax.random.split(jax.random.key(seed), 22)
    inputs = normal_values(seeds[0], (TOTAL_TOKENS, MODEL_DIMENSION), 1.0, 6.0, ((0, 128),))
    route_ids_keys = jax.random.split(jax.random.fold_in(seeds[1], 1), TOTAL_TOKENS // TOK_DEV)
    route_ids_turns = jax.random.permutation(jax.random.fold_in(seeds[1], 3), TOTAL_TOKENS // TOK_DEV)
    route_ids = jax.vmap(lambda own, number: shared_out(jax.random.fold_in(seeds[1], 2), own, number, TOK_DEV, EXPERTS, TOP, CAP, 2))(route_ids_keys, route_ids_turns).reshape((TOTAL_TOKENS, TOP))
    cotangent = normal_values(seeds[2], (TOTAL_TOKENS, MODEL_DIMENSION), 1.0, 6.0, ((0, 128),))
    query_key_value_weight = normal_values(seeds[3], (MODEL_DIMENSION, (QUERY_HEAD_COUNT + 2 * KEY_VALUE_HEADS) * HEAD_DIMENSION), (MODEL_DIMENSION // 2) ** -0.5, 0.25, ((0, 128),), jnp.float32)
    projection_first_moment = normal_values(seeds[4], (MODEL_DIMENSION, (QUERY_HEAD_COUNT + 2 * KEY_VALUE_HEADS) * HEAD_DIMENSION), (0.11 * TOTAL_TOKENS ** 0.5), 80.0, ((0, 128),), jnp.float32)
    projection_second_moment = jnp.clip(jnp.exp(math.log(6881.28) - 2.7821581 * jax.random.uniform(seeds[5], (MODEL_DIMENSION, (QUERY_HEAD_COUNT + 2 * KEY_VALUE_HEADS) * HEAD_DIMENSION), jnp.float32) ** steps_of(seeds[5], (MODEL_DIMENSION, (QUERY_HEAD_COUNT + 2 * KEY_VALUE_HEADS) * HEAD_DIMENSION), ((0, 128),), -0.2, 0.2)), 425.984, 6881.28)
    out_weight = normal_values(seeds[6], (QUERY_HEAD_COUNT * HEAD_DIMENSION, MODEL_DIMENSION), (QUERY_HEAD_COUNT * HEAD_DIMENSION // 4) ** -0.5, 0.375, ((0, 128),), jnp.float32)
    out_moment_one = normal_values(seeds[7], (QUERY_HEAD_COUNT * HEAD_DIMENSION, MODEL_DIMENSION), (0.066 * TOTAL_TOKENS ** 0.5), 48.0, ((0, 128),), jnp.float32)
    out_moment_two = jnp.clip(jnp.exp(math.log(2457.6) - 2.7593436 * jax.random.uniform(seeds[8], (QUERY_HEAD_COUNT * HEAD_DIMENSION, MODEL_DIMENSION), jnp.float32) ** steps_of(seeds[8], (QUERY_HEAD_COUNT * HEAD_DIMENSION, MODEL_DIMENSION), ((0, 128),), -0.2, 0.2)), 155.648, 2457.6)
    router_weight = normal_values(seeds[9], (MODEL_DIMENSION, EXPERTS), (4 * MODEL_DIMENSION) ** -0.5, 0.09375, ((0, 128),), jnp.float32)
    router_moment_one = normal_values(seeds[10], (MODEL_DIMENSION, EXPERTS), (0.033 * (MODEL_DIMENSION * TOTAL_TOKENS * TOP // EXPERTS) ** 0.5), 384.0, ((0, 128),), jnp.float32)
    router_moment_two = jnp.clip(jnp.exp(math.log(159383.55) - 2.804677 * jax.random.uniform(seeds[11], (MODEL_DIMENSION, EXPERTS), jnp.float32) ** steps_of(seeds[11], (MODEL_DIMENSION, EXPERTS), ((0, 128),), -0.2, 0.2)), 9646.899, 159383.55)
    gain_weight = jnp.clip(1.0 + 0.1 * jax.random.normal(seeds[12], (MODEL_DIMENSION, 2), jnp.float32), 0.5, 1.5)
    gain_moment_one = normal_values(seeds[13], (MODEL_DIMENSION, 2), (0.22 * TOTAL_TOKENS ** 0.5), 160.0, ((0, 128),), jnp.float32)
    gain_moment_two = jnp.clip(jnp.exp(math.log(27852.8) - 2.8332134 * jax.random.uniform(seeds[14], (MODEL_DIMENSION, 2), jnp.float32) ** steps_of(seeds[14], (MODEL_DIMENSION, 2), ((0, 128),), -0.2, 0.2)), 1638.4, 27852.8)
    expand_weight = normal_values(seeds[15], (EXPERTS, MODEL_DIMENSION, 2 * FF), MODEL_DIMENSION ** -0.5, 0.1875, ((0, 32), (1, 4)), jnp.float32)
    expand_moment_one = normal_values(seeds[16], (EXPERTS, MODEL_DIMENSION, 2 * FF), (0.055 * (TOTAL_TOKENS * TOP // EXPERTS) ** 0.5), 20.0, ((0, 32), (1, 4)), jnp.float32)
    expand_moment_two = jnp.clip(jnp.exp(math.log(430.08) - 2.7821581 * jax.random.uniform(seeds[17], (EXPERTS, MODEL_DIMENSION, 2 * FF), jnp.float32) ** steps_of(seeds[17], (EXPERTS, MODEL_DIMENSION, 2 * FF), ((0, 32), (1, 4)), -0.2, 0.2)), 26.624, 430.08)
    reduce_weight = normal_values(seeds[18], (EXPERTS, FF, MODEL_DIMENSION), (FF // 16) ** -0.5, 1.0, ((0, 32), (1, 4)), jnp.float32)
    reduce_moment_one = normal_values(seeds[19], (EXPERTS, FF, MODEL_DIMENSION), (0.0083 * (TOTAL_TOKENS * TOP // EXPERTS) ** 0.5), 3.0, ((0, 32), (1, 4)), jnp.float32)
    reduce_moment_two = jnp.clip(jnp.exp(math.log(9.8304) - 2.7725887 * jax.random.uniform(seeds[20], (EXPERTS, FF, MODEL_DIMENSION), jnp.float32) ** steps_of(seeds[20], (EXPERTS, FF, MODEL_DIMENSION), ((0, 32), (1, 4)), -0.2, 0.2)), 0.6144, 9.8304)
    return {"inputs": inputs, "route_ids": route_ids, "cotangent": cotangent, "query_key_value_weight": query_key_value_weight, "projection_first_moment": projection_first_moment, "projection_second_moment": projection_second_moment, "out_weight": out_weight, "out_moment_one": out_moment_one, "out_moment_two": out_moment_two, "router_weight": router_weight, "router_moment_one": router_moment_one, "router_moment_two": router_moment_two, "gain_weight": gain_weight, "gain_moment_one": gain_moment_one, "gain_moment_two": gain_moment_two, "expand_weight": expand_weight, "expand_moment_one": expand_moment_one, "expand_moment_two": expand_moment_two, "reduce_weight": reduce_weight, "reduce_moment_one": reduce_moment_one, "reduce_moment_two": reduce_moment_two}


@jax.custom_vjp
def lower_precision(v):
    return lax.optimization_barrier(v.astype(jnp.bfloat16)).astype(jnp.float32)

@jax.custom_vjp
def low_back(v):
    return v

def low_keep(v):
    return (lower_precision(v), None)

def low_pass(kept, grad):
    return (grad,)

def back_keep(v):
    return (v, None)

def back_low(kept, grad):
    return (lower_precision(grad),)
lower_precision.defvjp(low_keep, low_pass)
low_back.defvjp(back_keep, back_low)
norm_eps = 1e-05
rope_base = 10000.0
masked_score = -1e+30
beta_one = 0.9
beta_two = 0.95
adam_eps = 1e-08
matrix_decay = 0.1
rate_inputs = 0.1
rate_output = 0.15
rate_router = 0.04
rate_gains = 0.6
rate_expand = 0.08
rate_reduce = 0.4

def product(left_op, right_op):
    return jnp.dot(left_op, right_op, precision=lax.Precision.HIGHEST, preferred_element_type=jnp.float32)

def normed(value_rows, gain_column):
    inverse = lax.rsqrt(lax.optimization_barrier(jnp.mean(value_rows * value_rows, axis=-1, keepdims=True)) + norm_eps)
    return value_rows * inverse * gain_column

def rope_tables(positions):
    half_width = HEAD_DIMENSION // 2
    inverse_freq = rope_base ** (-(jnp.arange(half_width, dtype=jnp.float32) * 2.0) / HEAD_DIMENSION)
    angles = positions[:, None] * inverse_freq[None, :]
    rotary_cosine = jnp.concatenate([jnp.cos(angles), jnp.cos(angles)], axis=-1)
    rotary_sine = jnp.concatenate([jnp.sin(angles), jnp.sin(angles)], axis=-1)
    return (rotary_cosine, rotary_sine)

def apply_rotary(value_rows, rotary_cosine, rotary_sine):
    half_width = value_rows.shape[-1] // 2
    turned = jnp.concatenate([-value_rows[..., half_width:], value_rows[..., :half_width]], axis=-1)
    return value_rows * rotary_cosine[:, None, :] + turned * rotary_sine[:, None, :]

def sequence_attention(query_key_value_rows):
    sequence_length = query_key_value_rows.shape[0]
    combined_heads = QUERY_HEAD_COUNT * HEAD_DIMENSION
    key_value_width = KEY_VALUE_HEADS * HEAD_DIMENSION
    positions = jnp.arange(sequence_length, dtype=jnp.int32).astype(jnp.float32)
    rotary_cosine, rotary_sine = rope_tables(positions)
    query_rows = lower_precision(apply_rotary(query_key_value_rows[:, :combined_heads].reshape(sequence_length, QUERY_HEAD_COUNT, HEAD_DIMENSION), rotary_cosine, rotary_sine))
    expanded_keys = lower_precision(apply_rotary(query_key_value_rows[:, combined_heads:combined_heads + key_value_width].reshape(sequence_length, KEY_VALUE_HEADS, HEAD_DIMENSION), rotary_cosine, rotary_sine))
    value_rows = lower_precision(query_key_value_rows[:, combined_heads + key_value_width:].reshape(sequence_length, KEY_VALUE_HEADS, HEAD_DIMENSION))
    query_head_rows = query_rows.reshape(sequence_length, KEY_VALUE_HEADS, QUERY_HEAD_COUNT // KEY_VALUE_HEADS, HEAD_DIMENSION)
    scores = low_back(jnp.einsum('tkgd,skd->kgts', query_head_rows, expanded_keys, precision=lax.Precision.HIGHEST) * HEAD_DIMENSION ** (-0.5))
    places = jnp.arange(sequence_length, dtype=jnp.int32)
    allowed = places[:, None] >= places[None, :]
    scores = jnp.where(allowed, scores, masked_score)
    attn_probs = lower_precision(jax.nn.softmax(scores, axis=-1))
    mixed = jnp.einsum('kgts,skd->tkgd', attn_probs, value_rows, precision=lax.Precision.HIGHEST)
    return mixed.reshape(sequence_length, combined_heads)

def slot_numbers(route_block, experts):
    flattened = route_block.reshape(-1)
    onehot = (flattened[:, None] == jnp.arange(experts, dtype=jnp.int32)[None, :]).astype(jnp.int32)
    earlier = jnp.cumsum(onehot, axis=0) - onehot
    return lax.optimization_barrier(jnp.sum(earlier * onehot, axis=1)).reshape(route_block.shape)

def experts_block(mixed_block, gate_block, route_block, expand_low, reduce_low):
    slot_index = slot_numbers(route_block, EXPERTS)
    token_index = jnp.broadcast_to(jnp.arange(TOK_DEV, dtype=jnp.int32)[:, None], (TOK_DEV, TOP))
    source_table = jnp.full((EXPERTS, CAP), TOK_DEV, dtype=jnp.int32)
    source_table = source_table.at[route_block.reshape(-1), slot_index.reshape(-1)].set(token_index.reshape(-1))
    padded = jnp.concatenate([mixed_block, jnp.zeros((1, MODEL_DIMENSION), dtype=jnp.float32)], axis=0)
    slot_rows = low_back(padded[source_table])
    gate_up = low_back(jnp.einsum('ecd,edf->ecf', slot_rows, expand_low, precision=lax.Precision.HIGHEST))
    hidden = lower_precision(jax.nn.silu(gate_up[..., :FF]) * gate_up[..., FF:])
    expert_out = low_back(lower_precision(jnp.einsum('ecf,efd->ecd', hidden, reduce_low, precision=lax.Precision.HIGHEST)))
    picked = expert_out[route_block, slot_index]
    return lax.optimization_barrier(jnp.sum(gate_block[..., None] * picked, axis=1))

def forward(route_ids, inputs, query_key_value_weight, out_weight, router_weight, gain_weight, expand_weight, reduce_weight):
    gain_low = lower_precision(gain_weight)
    attend_in = lower_precision(normed(inputs, gain_low[:, 0]))
    query_key_value_rows = low_back(product(attend_in, lower_precision(query_key_value_weight)))
    attention_output = lax.map(jax.checkpoint(sequence_attention), query_key_value_rows.reshape(N_EXPERT, SEQUENCE_TOKENS, (QUERY_HEAD_COUNT + 2 * KEY_VALUE_HEADS) * HEAD_DIMENSION))
    attention_output = low_back(lower_precision(attention_output.reshape(TOTAL_TOKENS, QUERY_HEAD_COUNT * HEAD_DIMENSION)))
    residual_state = inputs + low_back(product(attention_output, lower_precision(out_weight)))
    mixed_in = lower_precision(normed(residual_state, gain_low[:, 1]))
    logits = low_back(product(mixed_in, lower_precision(router_weight)))
    gate_values = jax.nn.softmax(jnp.take_along_axis(logits, route_ids, axis=1), axis=-1)
    expand_low = lower_precision(expand_weight)
    reduce_low = lower_precision(reduce_weight)

    def block_apply(pieces):
        return experts_block(pieces[0], pieces[1], pieces[2], expand_low, reduce_low)
    blocks = N_EXPERT * N_SHARD
    expert_sum = lax.map(jax.checkpoint(block_apply), (mixed_in.reshape(blocks, TOK_DEV, MODEL_DIMENSION), gate_values.reshape(blocks, TOK_DEV, TOP), route_ids.reshape(blocks, TOK_DEV, TOP)))
    return residual_state + expert_sum.reshape(TOTAL_TOKENS, MODEL_DIMENSION)

def adamw(weight, gradient, moment_one, moment_two, step_rate, decay_rate):
    one_new = beta_one * moment_one + (1.0 - beta_one) * gradient
    two_new = beta_two * moment_two + (1.0 - beta_two) * gradient * gradient
    one_hat = one_new / (1.0 - beta_one ** STEP)
    two_hat = two_new / (1.0 - beta_two ** STEP)
    weight_new = weight - step_rate * (one_hat / (jnp.sqrt(two_hat) + adam_eps) + decay_rate * weight)
    return (one_new, two_new, weight_new)

def reference(inputs, route_ids, cotangent, query_key_value_weight, projection_first_moment, projection_second_moment, out_weight, out_moment_one, out_moment_two, router_weight, router_moment_one, router_moment_two, gain_weight, gain_moment_one, gain_moment_two, expand_weight, expand_moment_one, expand_moment_two, reduce_weight, reduce_moment_one, reduce_moment_two):
    result, pullback = jax.vjp(partial(forward, route_ids), inputs.astype(jnp.float32), query_key_value_weight, out_weight, router_weight, gain_weight, expand_weight, reduce_weight)
    gradients = pullback(cotangent.astype(jnp.float32))
    qkv_one, qkv_two, qkv_new = adamw(query_key_value_weight, gradients[1], projection_first_moment, projection_second_moment, rate_inputs, matrix_decay)
    out_one, out_two, out_new = adamw(out_weight, gradients[2], out_moment_one, out_moment_two, rate_output, matrix_decay)
    router_one, router_two, router_new = adamw(router_weight, gradients[3], router_moment_one, router_moment_two, rate_router, matrix_decay)
    gain_one, gain_two, gain_new = adamw(gain_weight, gradients[4], gain_moment_one, gain_moment_two, rate_gains, 0.0)
    expand_one, expand_two, expand_new = adamw(expand_weight, gradients[5], expand_moment_one, expand_moment_two, rate_expand, matrix_decay)
    reduce_one, reduce_two, reduce_new = adamw(reduce_weight, gradients[6], reduce_moment_one, reduce_moment_two, rate_reduce, matrix_decay)
    return (result.astype(jnp.bfloat16), gradients[0], qkv_one, qkv_two, qkv_new, out_one, out_two, out_new, router_one, router_two, router_new, gain_one, gain_two, gain_new, expand_one, expand_two, expand_new, reduce_one, reduce_two, reduce_new)
```

```python
import jax
import jax.numpy as jnp
from jax import lax
from jax.sharding import PartitionSpec as P

D_MODEL = 1024
HEADS = 16
KV_HEADS = 8
HEAD = 64
FF = 512
TOP = 8
STEP = 10
CAP = 48
BOTH = ("expert", "shard")

norm_eps = 1e-05
rope_base = 10000.0
masked_score = -1e30
beta_one = 0.9
beta_two = 0.95
adam_eps = 1e-08
matrix_decay = 0.1
rate_inputs = 0.1
rate_output = 0.15
rate_router = 0.04
rate_gains = 0.6
rate_expand = 0.08
rate_reduce = 0.4

bf = jnp.bfloat16
f32 = jnp.float32
HIGHEST = lax.Precision.HIGHEST


def dot(a, b):
    return jnp.dot(a, b, preferred_element_type=f32)


def dot_tn(a, b):
    return lax.dot_general(a, b, (((0,), (0,)), ((), ())), preferred_element_type=f32)


def dot_nt(a, b):
    return lax.dot_general(a, b, (((1,), (1,)), ((), ())), preferred_element_type=f32)


def adamw(weight, gradient, moment_one, moment_two, step_rate, decay_rate):
    one_new = beta_one * moment_one + (1.0 - beta_one) * gradient
    two_new = beta_two * moment_two + (1.0 - beta_two) * gradient * gradient
    one_hat = one_new / (1.0 - beta_one**STEP)
    two_hat = two_new / (1.0 - beta_two**STEP)
    weight_new = weight - step_rate * (
        one_hat / (jnp.sqrt(two_hat) + adam_eps) + decay_rate * weight
    )
    return (one_new, two_new, weight_new)


def shift(block, size, amount):
    return lax.ppermute(block, "shard", [(i, (i + amount) % size) for i in range(size)])


def rotary(rows, cosine, sine):
    half = rows.shape[-1] // 2
    turned = jnp.concatenate([-rows[..., half:], rows[..., :half]], axis=-1)
    return rows * cosine[:, None, :] + turned * sine[:, None, :]


def rotary_back(grad, cosine, sine):
    half = grad.shape[-1] // 2
    scaled = grad * sine[:, None, :]
    turned = jnp.concatenate([scaled[..., half:], -scaled[..., :half]], axis=-1)
    return grad * cosine[:, None, :] + turned


def split_columns(rows, shards):
    n = rows.shape[0]
    q, k, v = jnp.split(rows, [HEADS * HEAD, (HEADS + KV_HEADS) * HEAD], axis=1)
    return jnp.concatenate(
        [q.reshape(n, shards, -1), k.reshape(n, shards, -1), v.reshape(n, shards, -1)], axis=2
    )


def join_columns(parts, shards):
    n = parts.shape[1]
    qw = HEADS * HEAD // shards
    kw = KV_HEADS * HEAD // shards
    moved = jnp.swapaxes(parts, 0, 1)
    return jnp.concatenate(
        [
            moved[:, :, :qw].reshape(n, -1),
            moved[:, :, qw : qw + kw].reshape(n, -1),
            moved[:, :, qw + kw :].reshape(n, -1),
        ],
        axis=1,
    )


def local(
    inputs,
    route_ids,
    cotangent,
    qkv_w,
    qkv_m,
    qkv_v,
    out_w,
    out_m,
    out_v,
    router_w,
    router_m,
    router_v,
    gain_w,
    gain_m,
    gain_v,
    expand_w,
    expand_m,
    expand_v,
    reduce_w,
    reduce_m,
    reduce_v,
):
    tokens = inputs.shape[0]
    experts = lax.axis_size("expert")
    shards = lax.axis_size("shard")
    devices = experts * shards
    own_rows = qkv_w.shape[0]
    slots = experts * CAP
    my_shard = lax.axis_index("shard")
    sequence = tokens * shards
    q_heads = HEADS // shards
    kv_heads = KV_HEADS // shards
    group = HEADS // KV_HEADS
    q_width = q_heads * HEAD
    kv_width = kv_heads * HEAD
    own_width = q_width + 2 * kv_width

    with jax.named_scope("weights_out"):
        extras = jnp.concatenate(
            [router_w, gain_w, jnp.zeros((own_rows, 128 - experts - 2), f32)], axis=1
        ).astype(bf)
        packed = jnp.concatenate(
            [
                split_columns(qkv_w.astype(bf), shards),
                jnp.broadcast_to(extras[:, None], (own_rows, shards, 128)),
            ],
            axis=2,
        )
        packed = jnp.broadcast_to(
            jnp.swapaxes(packed, 0, 1)[None], (experts, shards, own_rows, own_width + 128)
        ).reshape(devices, own_rows, own_width + 128)
        weights = lax.all_to_all(packed, BOTH, 0, 0, tiled=True).reshape(D_MODEL, own_width + 128)
    out_full = lax.all_gather(out_w.astype(bf), BOTH, axis=0, tiled=True)
    sequence_rows = jnp.concatenate(
        [inputs] + [shift(inputs, shards, k) for k in range(1, shards)], axis=0
    )
    expand_full = lax.all_gather(expand_w.astype(bf), "shard", axis=1, tiled=True)[0]
    reduce_full = lax.all_gather(reduce_w.astype(bf), "shard", axis=1, tiled=True)[0]

    with jax.named_scope("routing"):
        expert_ids = jnp.arange(experts, dtype=jnp.int32)
        chosen = jnp.any(route_ids[:, :, None] == expert_ids[None, None, :], axis=1)
        chosen_b = chosen.astype(bf)
        token_ids = jnp.arange(tokens, dtype=jnp.int32)
        earlier = (token_ids[:, None] > token_ids[None, :]).astype(bf)
        place = jnp.where(chosen, dot(earlier, chosen_b), -1.0).astype(bf)
        slot_ids = jnp.arange(slots, dtype=jnp.int32)
        spread = (slot_ids[None, :] // CAP == expert_ids[:, None]).astype(bf)
        place_of = dot(place, spread)
        select = (place_of == (slot_ids % CAP).astype(f32)[None, :]).astype(bf)

    with jax.named_scope("cotangent_out"):
        grad_sent = dot_tn(select, cotangent).astype(bf).reshape(experts, CAP, D_MODEL)
        grad_rows = lax.all_to_all(grad_sent, "expert", 0, 0, tiled=True).reshape(slots, D_MODEL)

    block_ids = (my_shard - jnp.arange(shards, dtype=jnp.int32) + shards) % shards
    positions = (block_ids[:, None] * tokens + token_ids[None, :]).reshape(-1)
    inverse_freq = rope_base ** (-(jnp.arange(HEAD // 2, dtype=f32) * 2.0) / HEAD)
    angles = positions.astype(f32)[:, None] * inverse_freq[None, :]
    cosine = jnp.concatenate([jnp.cos(angles), jnp.cos(angles)], axis=-1)
    sine = jnp.concatenate([jnp.sin(angles), jnp.sin(angles)], axis=-1)
    allowed = positions[:, None] >= positions[None, :]

    with jax.named_scope("attention_in"):
        wide = sequence_rows.astype(f32)
        inverse_one = lax.rsqrt(jnp.mean(wide * wide, axis=-1, keepdims=True) + norm_eps)
        normal_one = wide * inverse_one
        qkv_own = weights[:, :own_width]
        router_full = weights[:, own_width : own_width + experts]
        gains = weights[:, own_width + experts : own_width + experts + 2].astype(f32)
        gain_one = gains[:, 0]
        gain_two = gains[:, 1]
        attend_in = (normal_one * gain_one).astype(bf)
        qkv = dot(attend_in, qkv_own)
        query = rotary(qkv[:, :q_width].reshape(sequence, q_heads, HEAD), cosine, sine)
        query = query.astype(bf).reshape(sequence, kv_heads, group, HEAD)
        keys = rotary(
            qkv[:, q_width : q_width + kv_width].reshape(sequence, kv_heads, HEAD), cosine, sine
        ).astype(bf)
        values = qkv[:, q_width + kv_width :].astype(bf).reshape(sequence, kv_heads, HEAD)

    with jax.named_scope("attention"):
        scale = HEAD ** (-0.5)
        scores = jnp.einsum("tkgd,skd->kgts", query, keys, preferred_element_type=f32) * scale
        scores = jnp.where(allowed, scores, masked_score)
        row_max = jnp.max(scores, axis=-1, keepdims=True)
        powers = jnp.exp(scores - row_max)
        probs = powers / jnp.sum(powers, axis=-1, keepdims=True)
        probs_b = probs.astype(bf)
        attended_own = jnp.einsum("kgts,skd->tkgd", probs_b, values, preferred_element_type=f32)
        attended_own = attended_own.astype(bf).reshape(sequence, q_width)

    def to_tokens(rows):
        return [rows[:tokens]] + [
            shift(rows[k * tokens : (k + 1) * tokens], shards, -k) for k in range(1, shards)
        ]

    def own_column_block(full, k):
        start = (my_shard + k) % shards * q_width
        return lax.dynamic_slice(full, (0, start), (full.shape[0], q_width))

    def own_row_block(full, k):
        start = (my_shard + k) % shards * q_width
        return lax.dynamic_slice(full, (start, 0), (q_width, full.shape[1]))

    with jax.named_scope("attention_out"):
        pieces = to_tokens(attended_own)
        attended = jnp.concatenate(pieces, axis=1)
        out_turned = jnp.concatenate([own_row_block(out_full, k) for k in range(shards)], axis=0)
        state = inputs.astype(f32) + dot(attended, out_turned)
        inverse_two = lax.rsqrt(jnp.mean(state * state, axis=-1, keepdims=True) + norm_eps)
        normal_two = state * inverse_two
        mixed_in = (normal_two * gain_two).astype(bf)

    with jax.named_scope("dispatch"):
        sent = dot_tn(select, mixed_in).astype(bf).reshape(experts, CAP, D_MODEL)
        rows = lax.all_to_all(sent, "expert", 0, 0, tiled=True).reshape(slots, D_MODEL)

    with jax.named_scope("gates"):
        logits = jnp.where(chosen, dot(mixed_in, router_full), masked_score)
        top_logit = jnp.max(logits, axis=-1, keepdims=True)
        gate_power = jnp.where(chosen, jnp.exp(logits - top_logit), 0.0)
        gates = gate_power / jnp.sum(gate_power, axis=-1, keepdims=True)
        gate_spread = jnp.dot(gates, spread.astype(f32), precision=HIGHEST)
        gate_select = gate_spread * select.astype(f32)
        gate_sent = jnp.sum(gate_select, axis=0).reshape(experts, CAP)
        gate_rows = lax.all_to_all(gate_sent, "expert", 0, 0, tiled=True).reshape(slots, 1)

    with jax.named_scope("experts"):
        hidden_grad = dot_nt(grad_rows, reduce_full)
        gate_up = dot(rows, expand_full)
        gate_part = gate_up[:, :FF]
        up_part = gate_up[:, FF:]
        sigmoid_gate = jax.nn.sigmoid(gate_part)
        silu_gate = gate_part * sigmoid_gate
        hidden = (silu_gate * up_part).astype(bf)
        hidden_gated = (hidden.astype(f32) * gate_rows).astype(bf)
        hidden_grad = hidden_grad * gate_rows
        gate_side = hidden_grad * up_part * sigmoid_gate * (1.0 + gate_part * (1.0 - sigmoid_gate))
        up_side = hidden_grad * silu_gate
        gate_up_grad = jnp.concatenate([gate_side, up_side], axis=1).astype(bf)
        row_grad = dot_nt(gate_up_grad, expand_full).astype(bf)
        rows_back = lax.all_to_all(
            row_grad.reshape(experts, CAP, D_MODEL), "expert", 0, 0, tiled=True
        ).reshape(slots, D_MODEL)
        produced = dot(hidden, reduce_full).astype(bf)
        gate_grad_rows = jnp.sum(produced.astype(f32) * grad_rows.astype(f32), axis=1)
        gate_grad_back = lax.all_to_all(
            gate_grad_rows.reshape(experts, CAP), "expert", 0, 0, tiled=True
        ).reshape(1, slots)
        returned = lax.all_to_all(
            produced.reshape(experts, CAP, D_MODEL), "expert", 0, 0, tiled=True
        ).reshape(slots, D_MODEL)
        reduce_grad = dot_tn(hidden_gated, grad_rows)
        expand_grad = dot_tn(rows, gate_up_grad)
        expand_sum = lax.psum_scatter(
            expand_grad[None].astype(bf), "shard", scatter_dimension=1, tiled=True
        ).astype(f32)
        reduce_sum = lax.psum_scatter(
            reduce_grad[None].astype(bf), "shard", scatter_dimension=1, tiled=True
        ).astype(f32)

    with jax.named_scope("outputs"):
        gate_high = gate_select.astype(bf)
        gate_low = (gate_select - gate_high.astype(f32)).astype(bf)
        outputs = (state + (dot(gate_high, returned) + dot(gate_low, returned))).astype(bf)

    with jax.named_scope("state_grad"):
        gate_grad = jnp.dot(
            select.astype(f32) * gate_grad_back, spread.astype(f32).T, precision=HIGHEST
        )
        mean_gate = jnp.sum(gates * gate_grad, axis=-1, keepdims=True)
        logit_grad = (gates * (gate_grad - mean_gate)).astype(bf)
        grad_out = cotangent.astype(f32)
        mixed_grad = dot(select, rows_back) + dot_nt(logit_grad, router_full)
        scaled_two = mixed_grad * gain_two
        gain_two_grad = jnp.sum(mixed_grad * normal_two, axis=0)
        state_grad = grad_out + inverse_two * (
            scaled_two - normal_two * jnp.mean(scaled_two * normal_two, axis=-1, keepdims=True)
        )
        branch_grad = state_grad.astype(bf)

    with jax.named_scope("attended_grad"):
        attended_grad = dot_nt(branch_grad, out_turned).astype(bf)
        grad_pieces = [attended_grad[:, :q_width]] + [
            shift(attended_grad[:, k * q_width : (k + 1) * q_width], shards, k)
            for k in range(1, shards)
        ]
        attended_grad_own = jnp.concatenate(grad_pieces, axis=0).reshape(
            sequence, kv_heads, group, HEAD
        )

    with jax.named_scope("out_grad"):
        attended_sorted = jnp.concatenate(
            [
                lax.dynamic_slice(
                    attended,
                    (0, (k - my_shard + shards) % shards * q_width),
                    (tokens, q_width),
                )
                for k in range(shards)
            ],
            axis=1,
        )
        out_grad = dot_tn(attended_sorted, branch_grad)
        router_grad = dot_tn(mixed_in, logit_grad)
        out_extras = jnp.concatenate(
            [router_grad, gain_two_grad[:, None], jnp.zeros((D_MODEL, 128 - experts - 1), f32)],
            axis=1,
        )
        out_sent = (
            jnp.concatenate([out_grad, out_extras], axis=1)
            .astype(bf)
            .reshape(devices, own_rows, D_MODEL + 128)
        )
        out_parts = lax.all_to_all(out_sent, BOTH, 0, 0, tiled=True)
        out_total = jnp.sum(out_parts.astype(f32), axis=0)
        out_sum = out_total[:, :D_MODEL]
        router_sum = out_total[:, D_MODEL : D_MODEL + experts]
        gain_two_sum = out_total[:, D_MODEL + experts : D_MODEL + experts + 1]

    with jax.named_scope("attention_grad"):
        prob_grad = jnp.einsum(
            "tkgd,skd->kgts", attended_grad_own, values, preferred_element_type=f32
        )
        row_dot = jnp.sum(probs * prob_grad, axis=-1, keepdims=True)
        score_grad = (probs * (prob_grad - row_dot)).astype(bf)
        query_grad = (
            jnp.einsum("kgts,skd->tkgd", score_grad, keys, preferred_element_type=f32) * scale
        )
        key_grad = (
            jnp.einsum("kgts,tkgd->skd", score_grad, query, preferred_element_type=f32) * scale
        )
        value_grad = jnp.einsum(
            "kgts,tkgd->skd", probs_b, attended_grad_own, preferred_element_type=f32
        )
        query_back = rotary_back(
            query_grad.reshape(sequence, q_heads, HEAD), cosine, sine
        ).reshape(sequence, q_width)
        key_back = rotary_back(key_grad, cosine, sine).reshape(sequence, kv_width)
        qkv_grad = jnp.concatenate(
            [query_back, key_back, value_grad.reshape(sequence, kv_width)], axis=1
        ).astype(bf)

    with jax.named_scope("qkv_grad"):
        attend_grad_part = dot_nt(qkv_grad, qkv_own)
        gain_one_grad = jnp.sum(attend_grad_part * normal_one, axis=0)
        qkv_wgrad = dot_tn(attend_in, qkv_grad)
        qkv_sent = (
            jnp.concatenate(
                [qkv_wgrad, gain_one_grad[:, None], jnp.zeros((D_MODEL, 127), f32)], axis=1
            )
            .astype(bf)
            .reshape(devices, own_rows, own_width + 128)
        )
        qkv_parts = lax.all_to_all(qkv_sent, BOTH, 0, 0, tiled=True)
        qkv_total = jnp.sum(
            qkv_parts.reshape(experts, shards, own_rows, own_width + 128).astype(f32), axis=0
        )
        qkv_sum = join_columns(qkv_total[:, :, :own_width], shards)
        gain_one_sum = jnp.sum(qkv_total[:, :, own_width : own_width + 1], axis=0)

    with jax.named_scope("input_grad"):
        attend_pieces = to_tokens(attend_grad_part.astype(bf))
        attend_grad = sum(piece.astype(f32) for piece in attend_pieces)
        own_normal = normal_one[:tokens]
        scaled_one = attend_grad * gain_one
        input_grad = state_grad + inverse_one[:tokens] * (
            scaled_one - own_normal * jnp.mean(scaled_one * own_normal, axis=-1, keepdims=True)
        )

    with jax.named_scope("update"):
        gain_sum = jnp.concatenate([gain_one_sum, gain_two_sum], axis=1)
        qkv_new = adamw(qkv_w, qkv_sum, qkv_m, qkv_v, rate_inputs, matrix_decay)
        out_new = adamw(out_w, out_sum, out_m, out_v, rate_output, matrix_decay)
        router_new = adamw(router_w, router_sum, router_m, router_v, rate_router, matrix_decay)
        gain_new = adamw(gain_w, gain_sum, gain_m, gain_v, rate_gains, 0.0)
        expand_new = adamw(expand_w, expand_sum, expand_m, expand_v, rate_expand, matrix_decay)
        reduce_new = adamw(reduce_w, reduce_sum, reduce_m, reduce_v, rate_reduce, matrix_decay)
    return (
        outputs,
        input_grad,
        *qkv_new,
        *out_new,
        *router_new,
        *gain_new,
        *expand_new,
        *reduce_new,
    )


def solution(mesh):
    rows = P(BOTH, None)
    expert = P("expert", "shard", None)
    return jax.shard_map(
        local,
        mesh=mesh,
        in_specs=(rows,) * 15 + (expert,) * 6,
        out_specs=(rows,) * 14 + (expert,) * 6,
        check_vma=False,
    )
```

```python
import jax
import jax.numpy as jnp
from jax import lax
from jax.sharding import Mesh
from jax.sharding import PartitionSpec as P

D_MODEL = 1024
HEADS = 16
KV_HEADS = 8
HEAD = 64
FF = 512
TOP = 8
STEP = 10
CAP = 48
EXPERT = ("plane", "core")
CHIPS = ("plane", "shard")
ALL = ("plane", "core", "shard")

norm_eps = 1e-05
rope_base = 10000.0
masked_score = -1e30
beta_one = 0.9
beta_two = 0.95
adam_eps = 1e-08
matrix_decay = 0.1
rate_inputs = 0.1
rate_output = 0.15
rate_router = 0.04
rate_gains = 0.6
rate_expand = 0.08
rate_reduce = 0.4

bf = jnp.bfloat16
f32 = jnp.float32
HIGHEST = lax.Precision.HIGHEST


def dot(a, b):
    return jnp.dot(a, b, preferred_element_type=f32)


def dot_tn(a, b):
    return lax.dot_general(a, b, (((0,), (0,)), ((), ())), preferred_element_type=f32)


def dot_nt(a, b):
    return lax.dot_general(a, b, (((1,), (1,)), ((), ())), preferred_element_type=f32)


def adamw(weight, gradient, moment_one, moment_two, step_rate, decay_rate):
    one_new = beta_one * moment_one + (1.0 - beta_one) * gradient
    two_new = beta_two * moment_two + (1.0 - beta_two) * gradient * gradient
    one_hat = one_new / (1.0 - beta_one**STEP)
    two_hat = two_new / (1.0 - beta_two**STEP)
    weight_new = weight - step_rate * (
        one_hat / (jnp.sqrt(two_hat) + adam_eps) + decay_rate * weight
    )
    return (one_new, two_new, weight_new)


def shift(block, size, amount):
    return lax.ppermute(block, "shard", [(i, (i + amount) % size) for i in range(size)])


def other_core(block):
    return lax.ppermute(block, "core", [(0, 1), (1, 0)])


def by_core(first, mine, other):
    return jnp.stack([jnp.where(first, mine, other), jnp.where(first, other, mine)], axis=1)


def after(value, *earlier):
    return lax.optimization_barrier((value, *earlier))


def rotary(rows, cosine, sine):
    half = rows.shape[-1] // 2
    turned = jnp.concatenate([-rows[..., half:], rows[..., :half]], axis=-1)
    return rows * cosine[:, None, :] + turned * sine[:, None, :]


def rotary_back(grad, cosine, sine):
    half = grad.shape[-1] // 2
    scaled = grad * sine[:, None, :]
    turned = jnp.concatenate([scaled[..., half:], -scaled[..., :half]], axis=-1)
    return grad * cosine[:, None, :] + turned


def split_columns(rows, shards):
    n = rows.shape[0]
    q, k, v = jnp.split(rows, [HEADS * HEAD, (HEADS + KV_HEADS) * HEAD], axis=1)
    return jnp.concatenate(
        [q.reshape(n, shards, -1), k.reshape(n, shards, -1), v.reshape(n, shards, -1)], axis=2
    )


def join_columns(parts, shards):
    n = parts.shape[1]
    qw = HEADS * HEAD // shards
    kw = KV_HEADS * HEAD // shards
    moved = jnp.swapaxes(parts, 0, 1)
    return jnp.concatenate(
        [
            moved[:, :, :qw].reshape(n, -1),
            moved[:, :, qw : qw + kw].reshape(n, -1),
            moved[:, :, qw + kw :].reshape(n, -1),
        ],
        axis=1,
    )


def local(
    inputs,
    route_ids,
    cotangent,
    qkv_w,
    qkv_m,
    qkv_v,
    out_w,
    out_m,
    out_v,
    router_w,
    router_m,
    router_v,
    gain_w,
    gain_m,
    gain_v,
    expand_w,
    expand_m,
    expand_v,
    reduce_w,
    reduce_m,
    reduce_v,
):
    tokens = inputs.shape[0]
    experts = lax.axis_size(EXPERT)
    shards = lax.axis_size("shard")
    planes = lax.axis_size("plane")
    first_core = lax.axis_index("core") == 0
    own_rows = qkv_w.shape[0]
    slots = experts * CAP
    my_shard = lax.axis_index("shard")
    sequence = tokens * shards
    q_heads = HEADS // shards
    kv_heads = KV_HEADS // shards
    group = HEADS // KV_HEADS
    q_width = q_heads * HEAD
    kv_width = kv_heads * HEAD
    own_width = q_width + 2 * kv_width

    width_out = D_MODEL
    out_fold = width_out * own_rows // (shards * own_rows)

    with jax.named_scope("weights_out"):
        extras = jnp.concatenate(
            [router_w, gain_w, jnp.zeros((own_rows, 128 - experts - 2), f32)], axis=1
        ).astype(bf)
        packed = jnp.concatenate(
            [
                split_columns(qkv_w.astype(bf), shards),
                jnp.broadcast_to(extras[:, None], (own_rows, shards, 128)),
            ],
            axis=2,
        )
        moves = [(s * experts + m, m * shards + s) for s in range(shards) for m in range(experts)]
        out_moved = lax.ppermute(out_w.astype(bf), ALL, moves)
        folds = width_out // out_fold
        out_moved = jnp.swapaxes(out_moved.reshape(own_rows, folds, out_fold), 0, 1)
        out_moved = out_moved.reshape(own_rows * folds, out_fold)
        packed = lax.all_to_all(jnp.swapaxes(packed, 0, 1), "shard", 0, 0, tiled=True)
        packed = packed.reshape(shards * own_rows, own_width + 128)
        packed = jnp.concatenate([packed, out_moved], axis=1)
        mine = lax.all_to_all(
            jnp.broadcast_to(packed[None], (planes, *packed.shape)), "plane", 0, 0, tiled=True
        )
    sequence_rows = jnp.concatenate(
        [inputs] + [shift(inputs, shards, k) for k in range(1, shards)], axis=0
    )
    expand_full = lax.all_gather(expand_w.astype(bf), "shard", axis=1, tiled=True)[0]
    reduce_full = lax.all_gather(reduce_w.astype(bf), "shard", axis=1, tiled=True)[0]

    with jax.named_scope("routing"):
        expert_ids = jnp.arange(experts, dtype=jnp.int32)
        chosen = jnp.any(route_ids[:, :, None] == expert_ids[None, None, :], axis=1)
        chosen_b = chosen.astype(bf)
        token_ids = jnp.arange(tokens, dtype=jnp.int32)
        earlier = (token_ids[:, None] > token_ids[None, :]).astype(bf)
        place = jnp.where(chosen, dot(earlier, chosen_b), -1.0).astype(bf)
        slot_ids = jnp.arange(slots, dtype=jnp.int32)
        spread = (slot_ids[None, :] // CAP == expert_ids[:, None]).astype(bf)
        place_of = dot(place, spread)
        select = (place_of == (slot_ids % CAP).astype(f32)[None, :]).astype(bf)

    with jax.named_scope("cotangent_out"):
        grad_sent = dot_tn(select, cotangent).astype(bf).reshape(experts, CAP, D_MODEL)
        grad_sent, mine = after(grad_sent, mine)
        grad_rows = lax.all_to_all(grad_sent, EXPERT, 0, 0, tiled=True).reshape(slots, D_MODEL)

    weights = by_core(first_core, mine, other_core(mine)).reshape(D_MODEL, -1)
    out_own = weights[:, own_width + 128 :].reshape(experts, folds, own_rows, out_fold)
    out_own = jnp.swapaxes(out_own, 1, 2).reshape(q_width, width_out)

    block_ids = (my_shard - jnp.arange(shards, dtype=jnp.int32) + shards) % shards
    positions = (block_ids[:, None] * tokens + token_ids[None, :]).reshape(-1)
    inverse_freq = rope_base ** (-(jnp.arange(HEAD // 2, dtype=f32) * 2.0) / HEAD)
    angles = positions.astype(f32)[:, None] * inverse_freq[None, :]
    cosine = jnp.concatenate([jnp.cos(angles), jnp.cos(angles)], axis=-1)
    sine = jnp.concatenate([jnp.sin(angles), jnp.sin(angles)], axis=-1)
    allowed = positions[:, None] >= positions[None, :]

    with jax.named_scope("attention_in"):
        wide = sequence_rows.astype(f32)
        inverse_one = lax.rsqrt(jnp.mean(wide * wide, axis=-1, keepdims=True) + norm_eps)
        normal_one = wide * inverse_one
        qkv_own = weights[:, :own_width]
        router_full = weights[:, own_width : own_width + experts]
        gains = weights[:, own_width + experts : own_width + experts + 2].astype(f32)
        gain_one = gains[:, 0]
        gain_two = gains[:, 1]
        attend_in = (normal_one * gain_one).astype(bf)
        qkv = dot(attend_in, qkv_own)
        query = rotary(qkv[:, :q_width].reshape(sequence, q_heads, HEAD), cosine, sine)
        query = query.astype(bf).reshape(sequence, kv_heads, group, HEAD)
        keys = rotary(
            qkv[:, q_width : q_width + kv_width].reshape(sequence, kv_heads, HEAD), cosine, sine
        ).astype(bf)
        values = qkv[:, q_width + kv_width :].astype(bf).reshape(sequence, kv_heads, HEAD)

    with jax.named_scope("attention"):
        scale = HEAD ** (-0.5)
        scores = jnp.einsum("tkgd,skd->kgts", query, keys, preferred_element_type=f32) * scale
        scores = jnp.where(allowed, scores, masked_score)
        row_max = jnp.max(scores, axis=-1, keepdims=True)
        powers = jnp.exp(scores - row_max)
        probs = powers / jnp.sum(powers, axis=-1, keepdims=True)
        probs_b = probs.astype(bf)
        attended_own = jnp.einsum("kgts,skd->tkgd", probs_b, values, preferred_element_type=f32)
        attended_own = attended_own.astype(bf).reshape(sequence, q_width)

    def to_tokens(rows):
        return [rows[:tokens]] + [
            shift(rows[k * tokens : (k + 1) * tokens], shards, -k) for k in range(1, shards)
        ]

    def rotate(blocks):
        start = (shards - my_shard) % shards * q_width
        return lax.dynamic_slice(
            jnp.concatenate([blocks, blocks], axis=1), (0, start), blocks.shape
        )

    def head_block(full, k):
        start = (my_shard + k) % shards * q_width
        return lax.dynamic_slice(full, (0, start), (full.shape[0], q_width))

    def split_rows(grad):
        parts = grad.reshape(planes, 2, grad.shape[0] // experts, -1)
        return (
            jnp.where(first_core, parts[:, 0], parts[:, 1]),
            jnp.where(first_core, parts[:, 1], parts[:, 0]),
        )

    def add_cores(keep, got):
        return (keep.astype(f32) + got.astype(f32)).astype(bf)

    def send_rows(total, axes):
        total = total.reshape(-1, own_rows, total.shape[-1])
        return lax.all_to_all(total, axes, 0, 0, tiled=True)

    with jax.named_scope("attention_out"):
        branch_part = dot(attended_own, out_own)
        pieces = to_tokens(branch_part.astype(bf))
        branch = branch_part[:tokens] + sum(piece.astype(f32) for piece in pieces[1:])
        state = inputs.astype(f32) + branch
        inverse_two = lax.rsqrt(jnp.mean(state * state, axis=-1, keepdims=True) + norm_eps)
        normal_two = state * inverse_two
        mixed_in = (normal_two * gain_two).astype(bf)

    with jax.named_scope("gates"):
        logits = jnp.where(chosen, dot(mixed_in, router_full), masked_score)
        top_logit = jnp.max(logits, axis=-1, keepdims=True)
        gate_power = jnp.where(chosen, jnp.exp(logits - top_logit), 0.0)
        gates = gate_power / jnp.sum(gate_power, axis=-1, keepdims=True)
        gate_spread = jnp.dot(gates, spread.astype(f32), precision=HIGHEST)
        gate_select = gate_spread * select.astype(f32)
        gates_high = gates.astype(bf)
        gates_low = (gates - gates_high.astype(f32)).astype(bf)
        gate_lanes = jnp.concatenate(
            [gates_high, gates_low, jnp.zeros((tokens, 128 - 2 * experts), bf)], axis=1
        )

    with jax.named_scope("dispatch"):
        sent = dot_tn(select, jnp.concatenate([mixed_in, gate_lanes], axis=1)).astype(bf)
        sent = sent.reshape(experts, CAP, D_MODEL + 128)
        sent, grad_rows = after(sent, grad_rows)
        attended_sent, sent = after(attended_own, sent)
        attended = rotate(jnp.concatenate(to_tokens(attended_sent), axis=1))
        out_full = lax.all_gather(out_own, "shard", axis=0, tiled=True)
        arrived = lax.all_to_all(sent, EXPERT, 0, 0, tiled=True).reshape(slots, D_MODEL + 128)
        lane = jnp.arange(128, dtype=jnp.int32)
        mine = (lane < 2 * experts) & (lane % experts == lax.axis_index(EXPERT))
        gate_rows = jnp.sum(
            jnp.where(mine, arrived[:, D_MODEL:].astype(f32), 0.0), axis=1, keepdims=True
        )

    with jax.named_scope("experts"):
        expand_padded = jnp.pad(expand_full, ((0, 128), (0, 0)))
        gate_up = dot(arrived, expand_padded)
        gate_part = gate_up[:, :FF]
        up_part = gate_up[:, FF:]
        sigmoid_gate = jax.nn.sigmoid(gate_part)
        silu_gate = gate_part * sigmoid_gate
        hidden = (silu_gate * up_part).astype(bf)
        produced = dot(hidden, reduce_full).astype(bf)
        returned = lax.all_to_all(
            produced.reshape(experts, CAP, D_MODEL), EXPERT, 0, 0, tiled=True
        ).reshape(slots, D_MODEL)
        grad_rows, gate_rows, produced = after(grad_rows, gate_rows, produced)
        hidden_grad = dot_nt(grad_rows, reduce_full)
        hidden_gated = (hidden.astype(f32) * gate_rows).astype(bf)
        hidden_grad = hidden_grad * gate_rows
        gate_side = hidden_grad * up_part * sigmoid_gate * (1.0 + gate_part * (1.0 - sigmoid_gate))
        up_side = hidden_grad * silu_gate
        gate_up_grad = jnp.concatenate([gate_side, up_side], axis=1).astype(bf)
        row_grad = dot_nt(gate_up_grad, expand_full).astype(bf).reshape(experts, CAP, D_MODEL)
        row_grad, returned, out_full = after(row_grad, returned, out_full)
        hidden_gated, arrived, returned = after(hidden_gated, arrived, returned)
        rows_back = lax.all_to_all(row_grad, EXPERT, 0, 0, tiled=True).reshape(slots, D_MODEL)
        reduce_grad = dot_tn(hidden_gated, grad_rows)
        expand_grad = dot_tn(arrived, gate_up_grad)[:D_MODEL].astype(bf)
        reduce_sum = lax.psum_scatter(
            reduce_grad[None].astype(bf), "shard", scatter_dimension=1, tiled=True
        )

    with jax.named_scope("outputs"):
        gate_high = gate_select.astype(bf)
        gate_low = (gate_select - gate_high.astype(f32)).astype(bf)
        outputs = (state + (dot(gate_high, returned) + dot(gate_low, returned))).astype(bf)
        rows_back, outputs, expand_grad = after(rows_back, outputs, expand_grad)
        expand_sum = lax.psum_scatter(
            expand_grad[None], "shard", scatter_dimension=1, tiled=True
        )

    with jax.named_scope("state_grad"):
        pair_dots = dot_nt(cotangent, returned) * select.astype(f32)
        gate_grad = jnp.dot(pair_dots, spread.astype(f32).T, precision=HIGHEST)
        mean_gate = jnp.sum(gates * gate_grad, axis=-1, keepdims=True)
        logit_grad = (gates * (gate_grad - mean_gate)).astype(bf)
        grad_out = cotangent.astype(f32)
        mixed_grad = dot(select, rows_back) + dot_nt(logit_grad, router_full)
        scaled_two = mixed_grad * gain_two
        gain_two_grad = jnp.sum(mixed_grad * normal_two, axis=0)
        state_grad = grad_out + inverse_two * (
            scaled_two - normal_two * jnp.mean(scaled_two * normal_two, axis=-1, keepdims=True)
        )
        branch_grad = state_grad.astype(bf)

    with jax.named_scope("out_grad"):
        attended_grad = dot_nt(branch_grad, out_full).astype(bf)
        attended_grad_own = jnp.concatenate(
            [head_block(attended_grad, 0)]
            + [shift(head_block(attended_grad, k), shards, k) for k in range(1, shards)],
            axis=0,
        ).reshape(sequence, kv_heads, group, HEAD)
        attended_grad, branch_later, logit_later = after(attended_grad, branch_grad, logit_grad)
        out_extras = jnp.concatenate(
            [
                dot_tn(mixed_in, logit_later),
                gain_two_grad[:, None],
                jnp.zeros((D_MODEL, 127 - experts), f32),
            ],
            axis=1,
        )
        out_sent = jnp.concatenate([dot_tn(attended, branch_later), out_extras], axis=1)
        out_keep, out_give = split_rows(out_sent.astype(bf))
        out_total = add_cores(out_keep, other_core(out_give))
        attended_grad_own, out_total = after(attended_grad_own, out_total)
        out_parts = send_rows(out_total, CHIPS)
        out_held = jnp.sum(out_parts.astype(f32), axis=0)
        out_sum = out_held[:, :D_MODEL]
        router_sum = out_held[:, D_MODEL : D_MODEL + experts]
        gain_two_sum = out_held[:, D_MODEL + experts : D_MODEL + experts + 1]

    with jax.named_scope("attention_grad"):
        prob_grad = jnp.einsum(
            "tkgd,skd->kgts", attended_grad_own, values, preferred_element_type=f32
        )
        row_dot = jnp.sum(probs * prob_grad, axis=-1, keepdims=True)
        score_grad = (probs * (prob_grad - row_dot)).astype(bf)
        query_grad = (
            jnp.einsum("kgts,skd->tkgd", score_grad, keys, preferred_element_type=f32) * scale
        )
        key_grad = (
            jnp.einsum("kgts,tkgd->skd", score_grad, query, preferred_element_type=f32) * scale
        )
        value_grad = jnp.einsum(
            "kgts,tkgd->skd", probs_b, attended_grad_own, preferred_element_type=f32
        )
        query_back = rotary_back(
            query_grad.reshape(sequence, q_heads, HEAD), cosine, sine
        ).reshape(sequence, q_width)
        key_back = rotary_back(key_grad, cosine, sine).reshape(sequence, kv_width)
        qkv_grad = jnp.concatenate(
            [query_back, key_back, value_grad.reshape(sequence, kv_width)], axis=1
        ).astype(bf)

    with jax.named_scope("qkv_grad"):
        qkv_keep, qkv_give = split_rows(dot_tn(attend_in, qkv_grad).astype(bf))
        qkv_part = add_cores(qkv_keep, other_core(qkv_give))
        qkv_grad, qkv_give = after(qkv_grad, qkv_give)
        attend_grad_part = dot_nt(qkv_grad, qkv_own)
        attend_grad_sent, expand_sum, reduce_sum, qkv_part, out_parts = after(
            attend_grad_part.astype(bf), expand_sum, reduce_sum, qkv_part, out_parts
        )
        qkv_parts = send_rows(qkv_part, CHIPS)
        qkv_total = jnp.sum(
            qkv_parts.reshape(planes, shards, own_rows, own_width).astype(f32), axis=0
        )
        qkv_sum = join_columns(qkv_total, shards)
        gain_one_sum = jnp.sum(
            qkv_w.astype(bf).astype(f32) * qkv_sum, axis=1, keepdims=True
        ) / gain_w[:, :1].astype(bf).astype(f32)
        gain_sum = jnp.concatenate([gain_one_sum, gain_two_sum], axis=1)

    with jax.named_scope("input_grad"):
        attend_pieces = to_tokens(attend_grad_sent)
        attend_grad = sum(piece.astype(f32) for piece in attend_pieces)
        own_normal = normal_one[:tokens]
        scaled_one = attend_grad * gain_one
        input_grad = state_grad + inverse_one[:tokens] * (
            scaled_one - own_normal * jnp.mean(scaled_one * own_normal, axis=-1, keepdims=True)
        )

    with jax.named_scope("update"):
        qkv_new = adamw(qkv_w, qkv_sum, qkv_m, qkv_v, rate_inputs, matrix_decay)
        out_new = adamw(out_w, out_sum, out_m, out_v, rate_output, matrix_decay)
        router_new = adamw(router_w, router_sum, router_m, router_v, rate_router, matrix_decay)
        gain_new = adamw(gain_w, gain_sum, gain_m, gain_v, rate_gains, 0.0)
        expand_new = adamw(expand_w, expand_sum.astype(f32), expand_m, expand_v, rate_expand, matrix_decay)
        reduce_new = adamw(reduce_w, reduce_sum.astype(f32), reduce_m, reduce_v, rate_reduce, matrix_decay)
    return (
        outputs,
        input_grad,
        *qkv_new,
        *out_new,
        *router_new,
        *gain_new,
        *expand_new,
        *reduce_new,
    )


def solution(mesh):
    experts, shards = mesh.shape["expert"], mesh.shape["shard"]
    split = Mesh(mesh.devices.reshape(experts // 2, 2, shards), ("plane", "core", "shard"))
    rows = P(("plane", "core", "shard"), None)
    expert = P(EXPERT, "shard", None)
    return jax.shard_map(
        local,
        mesh=split,
        in_specs=(rows,) * 15 + (expert,) * 6,
        out_specs=(rows,) * 14 + (expert,) * 6,
        check_vma=False,
    )
```

```python
import jax
import jax.numpy as jnp
from jax import lax
from jax.sharding import Mesh
from jax.sharding import PartitionSpec as P

D_MODEL = 1024
HEADS = 16
KV_HEADS = 8
HEAD = 64
FF = 512
TOP = 8
STEP = 10
CAP = 48
EXPERT = ("plane", "core")
CHIPS = ("plane", "shard")
ALL = ("plane", "core", "shard")

norm_eps = 1e-05
rope_base = 10000.0
masked_score = -1e30
beta_one = 0.9
beta_two = 0.95
adam_eps = 1e-08
matrix_decay = 0.1
rate_inputs = 0.1
rate_output = 0.15
rate_router = 0.04
rate_gains = 0.6
rate_expand = 0.08
rate_reduce = 0.4

bf = jnp.bfloat16
f32 = jnp.float32
HIGHEST = lax.Precision.HIGHEST


def dot(a, b):
    return jnp.dot(a, b, preferred_element_type=f32)


def dot_tn(a, b):
    return lax.dot_general(a, b, (((0,), (0,)), ((), ())), preferred_element_type=f32)


def dot_nt(a, b):
    return lax.dot_general(a, b, (((1,), (1,)), ((), ())), preferred_element_type=f32)


def adamw(weight, gradient, moment_one, moment_two, step_rate, decay_rate):
    one_new = beta_one * moment_one + (1.0 - beta_one) * gradient
    two_new = beta_two * moment_two + (1.0 - beta_two) * gradient * gradient
    one_hat = one_new / (1.0 - beta_one**STEP)
    two_hat = two_new / (1.0 - beta_two**STEP)
    weight_new = weight - step_rate * (
        one_hat / (jnp.sqrt(two_hat) + adam_eps) + decay_rate * weight
    )
    return (one_new, two_new, weight_new)


def shift(block, size, amount):
    return lax.ppermute(block, "shard", [(i, (i + amount) % size) for i in range(size)])


def other_core(block):
    return lax.ppermute(block, "core", [(0, 1), (1, 0)])


def by_core(first, mine, other):
    return jnp.stack([jnp.where(first, mine, other), jnp.where(first, other, mine)], axis=1)


def after(value, *earlier):
    return lax.optimization_barrier((value, *earlier))


def rotary(rows, cosine, sine):
    half = rows.shape[-1] // 2
    turned = jnp.concatenate([-rows[..., half:], rows[..., :half]], axis=-1)
    return rows * cosine[:, None, :] + turned * sine[:, None, :]


def rotary_back(grad, cosine, sine):
    half = grad.shape[-1] // 2
    scaled = grad * sine[:, None, :]
    turned = jnp.concatenate([scaled[..., half:], -scaled[..., :half]], axis=-1)
    return grad * cosine[:, None, :] + turned


def split_columns(rows, shards):
    n = rows.shape[0]
    q, k, v = jnp.split(rows, [HEADS * HEAD, (HEADS + KV_HEADS) * HEAD], axis=1)
    return jnp.concatenate(
        [q.reshape(n, shards, -1), k.reshape(n, shards, -1), v.reshape(n, shards, -1)], axis=2
    )


def join_columns(parts, shards):
    n = parts.shape[1]
    qw = HEADS * HEAD // shards
    kw = KV_HEADS * HEAD // shards
    moved = jnp.swapaxes(parts, 0, 1)
    return jnp.concatenate(
        [
            moved[:, :, :qw].reshape(n, -1),
            moved[:, :, qw : qw + kw].reshape(n, -1),
            moved[:, :, qw + kw :].reshape(n, -1),
        ],
        axis=1,
    )


def local(
    inputs,
    route_ids,
    cotangent,
    qkv_w,
    qkv_m,
    qkv_v,
    out_w,
    out_m,
    out_v,
    router_w,
    router_m,
    router_v,
    gain_w,
    gain_m,
    gain_v,
    expand_w,
    expand_m,
    expand_v,
    reduce_w,
    reduce_m,
    reduce_v,
):
    tokens = inputs.shape[0]
    experts = lax.axis_size(EXPERT)
    shards = lax.axis_size("shard")
    planes = lax.axis_size("plane")
    first_core = lax.axis_index("core") == 0
    own_rows = qkv_w.shape[0]
    slots = experts * CAP
    my_shard = lax.axis_index("shard")
    sequence = tokens * shards
    q_heads = HEADS // shards
    kv_heads = KV_HEADS // shards
    group = HEADS // KV_HEADS
    q_width = q_heads * HEAD
    kv_width = kv_heads * HEAD
    own_width = q_width + 2 * kv_width

    width_out = D_MODEL
    out_fold = width_out * own_rows // (shards * own_rows)

    with jax.named_scope("weights_out"):
        extras = jnp.concatenate(
            [router_w, gain_w, jnp.zeros((own_rows, 128 - experts - 2), f32)], axis=1
        ).astype(bf)
        packed = jnp.concatenate(
            [
                split_columns(qkv_w.astype(bf), shards),
                jnp.broadcast_to(extras[:, None], (own_rows, shards, 128)),
            ],
            axis=2,
        )
        moves = [(s * experts + m, m * shards + s) for s in range(shards) for m in range(experts)]
        out_moved = lax.ppermute(out_w.astype(bf), ALL, moves)
        folds = width_out // out_fold
        out_moved = jnp.swapaxes(out_moved.reshape(own_rows, folds, out_fold), 0, 1)
        out_moved = out_moved.reshape(own_rows * folds, out_fold)
        packed = lax.all_to_all(jnp.swapaxes(packed, 0, 1), "shard", 0, 0, tiled=True)
        packed = packed.reshape(shards * own_rows, own_width + 128)
        packed = jnp.concatenate([packed, out_moved], axis=1)
        mine = lax.all_to_all(
            jnp.broadcast_to(packed[None], (planes, *packed.shape)), "plane", 0, 0, tiled=True
        )
    sequence_rows = jnp.concatenate(
        [inputs] + [shift(inputs, shards, k) for k in range(1, shards)], axis=0
    )
    expand_full = lax.all_gather(expand_w.astype(bf), "shard", axis=1, tiled=True)[0]
    reduce_full = lax.all_gather(reduce_w.astype(bf), "shard", axis=1, tiled=True)[0]

    with jax.named_scope("routing"):
        expert_ids = jnp.arange(experts, dtype=jnp.int32)
        chosen = jnp.any(route_ids[:, :, None] == expert_ids[None, None, :], axis=1)
        chosen_b = chosen.astype(bf)
        token_ids = jnp.arange(tokens, dtype=jnp.int32)
        earlier = (token_ids[:, None] > token_ids[None, :]).astype(bf)
        place = jnp.where(chosen, dot(earlier, chosen_b), -1.0).astype(bf)
        slot_ids = jnp.arange(slots, dtype=jnp.int32)
        spread = (slot_ids[None, :] // CAP == expert_ids[:, None]).astype(bf)
        place_of = dot(place, spread)
        select = (place_of == (slot_ids % CAP).astype(f32)[None, :]).astype(bf)

    with jax.named_scope("cotangent_out"):
        grad_sent = dot_tn(select, cotangent).astype(bf).reshape(experts, CAP, D_MODEL)
        grad_sent, mine = after(grad_sent, mine)
        grad_rows = lax.all_to_all(grad_sent, EXPERT, 0, 0, tiled=True).reshape(slots, D_MODEL)

    weights = by_core(first_core, mine, other_core(mine)).reshape(D_MODEL, -1)
    out_own = weights[:, own_width + 128 :].reshape(experts, folds, own_rows, out_fold)
    out_own = jnp.swapaxes(out_own, 1, 2).reshape(q_width, width_out)

    block_ids = (my_shard - jnp.arange(shards, dtype=jnp.int32) + shards) % shards
    positions = (block_ids[:, None] * tokens + token_ids[None, :]).reshape(-1)
    inverse_freq = rope_base ** (-(jnp.arange(HEAD // 2, dtype=f32) * 2.0) / HEAD)
    angles = positions.astype(f32)[:, None] * inverse_freq[None, :]
    cosine = jnp.concatenate([jnp.cos(angles), jnp.cos(angles)], axis=-1)
    sine = jnp.concatenate([jnp.sin(angles), jnp.sin(angles)], axis=-1)
    allowed = positions[:, None] >= positions[None, :]

    with jax.named_scope("attention_in"):
        wide = sequence_rows.astype(f32)
        inverse_one = lax.rsqrt(jnp.mean(wide * wide, axis=-1, keepdims=True) + norm_eps)
        normal_one = wide * inverse_one
        qkv_own = weights[:, :own_width]
        router_full = weights[:, own_width : own_width + experts]
        gains = weights[:, own_width + experts : own_width + experts + 2].astype(f32)
        gain_one = gains[:, 0]
        gain_two = gains[:, 1]
        attend_in = (normal_one * gain_one).astype(bf)
        qkv = dot(attend_in, qkv_own)
        query = rotary(qkv[:, :q_width].reshape(sequence, q_heads, HEAD), cosine, sine)
        query = query.astype(bf).reshape(sequence, kv_heads, group, HEAD)
        keys = rotary(
            qkv[:, q_width : q_width + kv_width].reshape(sequence, kv_heads, HEAD), cosine, sine
        ).astype(bf)
        values = qkv[:, q_width + kv_width :].astype(bf).reshape(sequence, kv_heads, HEAD)

    with jax.named_scope("attention"):
        scale = HEAD ** (-0.5)
        scores = jnp.einsum("tkgd,skd->kgts", query, keys, preferred_element_type=f32) * scale
        scores = jnp.where(allowed, scores, masked_score)
        row_max = jnp.max(scores, axis=-1, keepdims=True)
        powers = jnp.exp(scores - row_max)
        probs = powers / jnp.sum(powers, axis=-1, keepdims=True)
        probs_b = probs.astype(bf)
        attended_own = jnp.einsum("kgts,skd->tkgd", probs_b, values, preferred_element_type=f32)
        attended_own = attended_own.astype(bf).reshape(sequence, q_width)

    def to_tokens(rows):
        return [rows[:tokens]] + [
            shift(rows[k * tokens : (k + 1) * tokens], shards, -k) for k in range(1, shards)
        ]

    def rotate(blocks):
        start = (shards - my_shard) % shards * q_width
        return lax.dynamic_slice(
            jnp.concatenate([blocks, blocks], axis=1), (0, start), blocks.shape
        )

    def head_block(full, k):
        start = (my_shard + k) % shards * q_width
        return lax.dynamic_slice(full, (0, start), (full.shape[0], q_width))

    def split_rows(grad):
        parts = grad.reshape(planes, 2, grad.shape[0] // experts, -1)
        return (
            jnp.where(first_core, parts[:, 0], parts[:, 1]),
            jnp.where(first_core, parts[:, 1], parts[:, 0]),
        )

    def add_cores(keep, got):
        return (keep.astype(f32) + got.astype(f32)).astype(bf)

    def send_rows(total, axes):
        total = total.reshape(-1, own_rows, total.shape[-1])
        return lax.all_to_all(total, axes, 0, 0, tiled=True)

    with jax.named_scope("attention_out"):
        branch_part = dot(attended_own, out_own)
        pieces = to_tokens(branch_part.astype(bf))
        branch = branch_part[:tokens] + sum(piece.astype(f32) for piece in pieces[1:])
        state = inputs.astype(f32) + branch
        inverse_two = lax.rsqrt(jnp.mean(state * state, axis=-1, keepdims=True) + norm_eps)
        normal_two = state * inverse_two
        mixed_in = (normal_two * gain_two).astype(bf)

    with jax.named_scope("gates"):
        logits = jnp.where(chosen, dot(mixed_in, router_full), masked_score)
        top_logit = jnp.max(logits, axis=-1, keepdims=True)
        gate_power = jnp.where(chosen, jnp.exp(logits - top_logit), 0.0)
        gates = gate_power / jnp.sum(gate_power, axis=-1, keepdims=True)
        gate_spread = jnp.dot(gates, spread.astype(f32), precision=HIGHEST)
        gate_select = gate_spread * select.astype(f32)
        gates_high = gates.astype(bf)
        gates_low = (gates - gates_high.astype(f32)).astype(bf)
        gate_lanes = jnp.concatenate(
            [gates_high, gates_low, jnp.zeros((tokens, 128 - 2 * experts), bf)], axis=1
        )

    with jax.named_scope("dispatch"):
        sent = dot_tn(select, jnp.concatenate([mixed_in, gate_lanes], axis=1)).astype(bf)
        sent = sent.reshape(experts, CAP, D_MODEL + 128)
        sent, grad_rows = after(sent, grad_rows)
        attended_sent, sent = after(attended_own, sent)
        attended = rotate(jnp.concatenate(to_tokens(attended_sent), axis=1))
        out_full = lax.all_gather(out_own, "shard", axis=0, tiled=True)
        arrived = lax.all_to_all(sent, EXPERT, 0, 0, tiled=True).reshape(slots, D_MODEL + 128)
        lane = jnp.arange(128, dtype=jnp.int32)
        mine = (lane < 2 * experts) & (lane % experts == lax.axis_index(EXPERT))
        gate_rows = jnp.sum(
            jnp.where(mine, arrived[:, D_MODEL:].astype(f32), 0.0), axis=1, keepdims=True
        )

    with jax.named_scope("experts"):
        expand_padded = jnp.pad(expand_full, ((0, 128), (0, 0)))
        gate_part = dot(arrived, expand_padded[:, :FF])
        up_part = dot(arrived, expand_padded[:, FF:])
        hidden = (gate_part * jax.nn.sigmoid(gate_part) * up_part).astype(bf)
        produced = dot(hidden, reduce_full).astype(bf)
        returned = lax.all_to_all(
            produced.reshape(experts, CAP, D_MODEL), EXPERT, 0, 0, tiled=True
        ).reshape(slots, D_MODEL)
        grad_rows, gate_rows, arrived, hidden, produced = after(
            grad_rows, gate_rows, arrived, hidden, produced
        )
        hidden_grad = dot_nt(grad_rows, reduce_full)
        gate_up = dot(arrived, expand_padded)
        gate_part = gate_up[:, :FF]
        up_part = gate_up[:, FF:]
        sigmoid_gate = jax.nn.sigmoid(gate_part)
        silu_gate = gate_part * sigmoid_gate
        hidden_gated = (hidden.astype(f32) * gate_rows).astype(bf)
        hidden_grad = hidden_grad * gate_rows
        gate_side = hidden_grad * up_part * sigmoid_gate * (1.0 + gate_part * (1.0 - sigmoid_gate))
        up_side = hidden_grad * silu_gate
        gate_up_grad = jnp.concatenate([gate_side, up_side], axis=1).astype(bf)
        row_grad = dot_nt(gate_up_grad, expand_full).astype(bf).reshape(experts, CAP, D_MODEL)
        row_grad, returned, out_full = after(row_grad, returned, out_full)
        hidden_gated, arrived, returned = after(hidden_gated, arrived, returned)
        rows_back = lax.all_to_all(row_grad, EXPERT, 0, 0, tiled=True).reshape(slots, D_MODEL)
        reduce_grad = dot_tn(hidden_gated, grad_rows)
        expand_grad = dot_tn(arrived, gate_up_grad)[:D_MODEL].astype(bf)
        reduce_sum = lax.psum_scatter(
            reduce_grad[None].astype(bf), "shard", scatter_dimension=1, tiled=True
        )

    with jax.named_scope("outputs"):
        gate_high = gate_select.astype(bf)
        gate_low = (gate_select - gate_high.astype(f32)).astype(bf)
        outputs = (state + (dot(gate_high, returned) + dot(gate_low, returned))).astype(bf)
        rows_back, outputs, expand_grad = after(rows_back, outputs, expand_grad)
        expand_sum = lax.psum_scatter(
            expand_grad[None], "shard", scatter_dimension=1, tiled=True
        )

    with jax.named_scope("state_grad"):
        pair_dots = dot_nt(cotangent, returned) * select.astype(f32)
        gate_grad = jnp.dot(pair_dots, spread.astype(f32).T, precision=HIGHEST)
        mean_gate = jnp.sum(gates * gate_grad, axis=-1, keepdims=True)
        logit_grad = (gates * (gate_grad - mean_gate)).astype(bf)
        grad_out = cotangent.astype(f32)
        mixed_grad = dot(select, rows_back) + dot_nt(logit_grad, router_full)
        scaled_two = mixed_grad * gain_two
        gain_two_grad = jnp.sum(mixed_grad * normal_two, axis=0)
        state_grad = grad_out + inverse_two * (
            scaled_two - normal_two * jnp.mean(scaled_two * normal_two, axis=-1, keepdims=True)
        )
        branch_grad = state_grad.astype(bf)

    with jax.named_scope("out_grad"):
        out_keep, out_give = split_rows(dot_tn(attended, branch_grad).astype(bf))
        branch_grad, out_give = after(branch_grad, out_give)
        attended_grad = dot_nt(branch_grad, out_full).astype(bf)
        attended_grad_own = jnp.concatenate(
            [head_block(attended_grad, 0)]
            + [shift(head_block(attended_grad, k), shards, k) for k in range(1, shards)],
            axis=0,
        ).reshape(sequence, kv_heads, group, HEAD)
        out_total = add_cores(out_keep, other_core(out_give))
        attended_grad_own, out_total = after(attended_grad_own, out_total)
        out_parts = send_rows(out_total, CHIPS)
        out_sum = jnp.sum(out_parts.astype(f32), axis=0)

    with jax.named_scope("attention_grad"):
        prob_grad = jnp.einsum(
            "tkgd,skd->kgts", attended_grad_own, values, preferred_element_type=f32
        )
        row_dot = jnp.sum(probs * prob_grad, axis=-1, keepdims=True)
        score_grad = (probs * (prob_grad - row_dot)).astype(bf)
        query_grad = (
            jnp.einsum("kgts,skd->tkgd", score_grad, keys, preferred_element_type=f32) * scale
        )
        key_grad = (
            jnp.einsum("kgts,tkgd->skd", score_grad, query, preferred_element_type=f32) * scale
        )
        value_grad = jnp.einsum(
            "kgts,tkgd->skd", probs_b, attended_grad_own, preferred_element_type=f32
        )
        query_back = rotary_back(
            query_grad.reshape(sequence, q_heads, HEAD), cosine, sine
        ).reshape(sequence, q_width)
        key_back = rotary_back(key_grad, cosine, sine).reshape(sequence, kv_width)
        qkv_grad = jnp.concatenate(
            [query_back, key_back, value_grad.reshape(sequence, kv_width)], axis=1
        ).astype(bf)

    with jax.named_scope("qkv_grad"):
        extras_grad = jnp.concatenate(
            [
                dot_tn(mixed_in, logit_grad),
                gain_two_grad[:, None],
                jnp.zeros((D_MODEL, 127 - experts), f32),
            ],
            axis=1,
        ).astype(bf)
        qkv_sent = jnp.concatenate(
            [dot_tn(attend_in, qkv_grad).astype(bf), extras_grad], axis=1
        )
        qkv_keep, qkv_give = split_rows(qkv_sent)
        qkv_grad, qkv_give = after(qkv_grad, qkv_give)
        attend_grad_part = dot_nt(qkv_grad, qkv_own)
        qkv_give, out_parts = after(qkv_give, out_parts)
        qkv_part = add_cores(qkv_keep, other_core(qkv_give))
        attend_grad_sent, expand_sum, reduce_sum, qkv_part = after(
            attend_grad_part.astype(bf), expand_sum, reduce_sum, qkv_part
        )
        qkv_parts = send_rows(qkv_part, CHIPS)
        qkv_total = jnp.sum(
            qkv_parts.reshape(planes, shards, own_rows, own_width + 128).astype(f32), axis=0
        )
        qkv_sum = join_columns(qkv_total[:, :, :own_width], shards)
        extras_sum = jnp.sum(qkv_total[:, :, own_width:], axis=0)
        router_sum = extras_sum[:, :experts]
        gain_two_sum = extras_sum[:, experts : experts + 1]
        gain_one_sum = jnp.sum(
            qkv_w.astype(bf).astype(f32) * qkv_sum, axis=1, keepdims=True
        ) / gain_w[:, :1].astype(bf).astype(f32)
        gain_sum = jnp.concatenate([gain_one_sum, gain_two_sum], axis=1)

    with jax.named_scope("input_grad"):
        attend_pieces = to_tokens(attend_grad_sent)
        attend_grad = sum(piece.astype(f32) for piece in attend_pieces)
        own_normal = normal_one[:tokens]
        scaled_one = attend_grad * gain_one
        input_grad = state_grad + inverse_one[:tokens] * (
            scaled_one - own_normal * jnp.mean(scaled_one * own_normal, axis=-1, keepdims=True)
        )

    with jax.named_scope("update"):
        qkv_new = adamw(qkv_w, qkv_sum, qkv_m, qkv_v, rate_inputs, matrix_decay)
        out_new = adamw(out_w, out_sum, out_m, out_v, rate_output, matrix_decay)
        router_new = adamw(router_w, router_sum, router_m, router_v, rate_router, matrix_decay)
        gain_new = adamw(gain_w, gain_sum, gain_m, gain_v, rate_gains, 0.0)
        expand_new = adamw(expand_w, expand_sum.astype(f32), expand_m, expand_v, rate_expand, matrix_decay)
        reduce_new = adamw(reduce_w, reduce_sum.astype(f32), reduce_m, reduce_v, rate_reduce, matrix_decay)
    return (
        outputs,
        input_grad,
        *qkv_new,
        *out_new,
        *router_new,
        *gain_new,
        *expand_new,
        *reduce_new,
    )


def solution(mesh):
    experts, shards = mesh.shape["expert"], mesh.shape["shard"]
    split = Mesh(mesh.devices.reshape(experts // 2, 2, shards), ("plane", "core", "shard"))
    rows = P(("plane", "core", "shard"), None)
    expert = P(EXPERT, "shard", None)
    return jax.shard_map(
        local,
        mesh=split,
        in_specs=(rows,) * 15 + (expert,) * 6,
        out_specs=(rows,) * 14 + (expert,) * 6,
        check_vma=False,
    )
```

```python
import jax
import jax.numpy as jnp
from jax import lax
from jax.sharding import Mesh
from jax.sharding import PartitionSpec as P

D_MODEL = 1024
HEADS = 16
KV_HEADS = 8
HEAD = 64
FF = 512
TOP = 8
STEP = 10
CAP = 48
EXPERT = ("plane", "core")
CHIPS = ("plane", "shard")
ALL = ("plane", "core", "shard")

norm_eps = 1e-05
rope_base = 10000.0
masked_score = -1e30
beta_one = 0.9
beta_two = 0.95
adam_eps = 1e-08
matrix_decay = 0.1
rate_inputs = 0.1
rate_output = 0.15
rate_router = 0.04
rate_gains = 0.6
rate_expand = 0.08
rate_reduce = 0.4

bf = jnp.bfloat16
f32 = jnp.float32
HIGHEST = lax.Precision.HIGHEST


def dot(a, b):
    return jnp.dot(a, b, preferred_element_type=f32)


def dot_tn(a, b):
    return lax.dot_general(a, b, (((0,), (0,)), ((), ())), preferred_element_type=f32)


def dot_nt(a, b):
    return lax.dot_general(a, b, (((1,), (1,)), ((), ())), preferred_element_type=f32)


def adamw(weight, gradient, moment_one, moment_two, step_rate, decay_rate):
    one_new = beta_one * moment_one + (1.0 - beta_one) * gradient
    two_new = beta_two * moment_two + (1.0 - beta_two) * gradient * gradient
    one_hat = one_new / (1.0 - beta_one**STEP)
    two_hat = two_new / (1.0 - beta_two**STEP)
    weight_new = weight - step_rate * (
        one_hat / (jnp.sqrt(two_hat) + adam_eps) + decay_rate * weight
    )
    return (one_new, two_new, weight_new)


def shift(block, size, amount):
    return lax.ppermute(block, "shard", [(i, (i + amount) % size) for i in range(size)])


def other_core(block):
    return lax.ppermute(block, "core", [(0, 1), (1, 0)])


def by_core(first, mine, other):
    return jnp.stack([jnp.where(first, mine, other), jnp.where(first, other, mine)], axis=1)


def after(value, *earlier):
    return lax.optimization_barrier((value, *earlier))


def rotary(rows, cosine, sine):
    half = rows.shape[-1] // 2
    turned = jnp.concatenate([-rows[..., half:], rows[..., :half]], axis=-1)
    return rows * cosine[:, None, :] + turned * sine[:, None, :]


def rotary_back(grad, cosine, sine):
    half = grad.shape[-1] // 2
    scaled = grad * sine[:, None, :]
    turned = jnp.concatenate([scaled[..., half:], -scaled[..., :half]], axis=-1)
    return grad * cosine[:, None, :] + turned


def split_columns(rows, shards):
    n = rows.shape[0]
    q, k, v = jnp.split(rows, [HEADS * HEAD, (HEADS + KV_HEADS) * HEAD], axis=1)
    return jnp.concatenate(
        [q.reshape(n, shards, -1), k.reshape(n, shards, -1), v.reshape(n, shards, -1)], axis=2
    )


def join_columns(parts, shards):
    n = parts.shape[1]
    qw = HEADS * HEAD // shards
    kw = KV_HEADS * HEAD // shards
    moved = jnp.swapaxes(parts, 0, 1)
    return jnp.concatenate(
        [
            moved[:, :, :qw].reshape(n, -1),
            moved[:, :, qw : qw + kw].reshape(n, -1),
            moved[:, :, qw + kw :].reshape(n, -1),
        ],
        axis=1,
    )


def local(
    inputs,
    route_ids,
    cotangent,
    qkv_w,
    qkv_m,
    qkv_v,
    out_w,
    out_m,
    out_v,
    router_w,
    router_m,
    router_v,
    gain_w,
    gain_m,
    gain_v,
    expand_w,
    expand_m,
    expand_v,
    reduce_w,
    reduce_m,
    reduce_v,
):
    tokens = inputs.shape[0]
    experts = lax.axis_size(EXPERT)
    shards = lax.axis_size("shard")
    planes = lax.axis_size("plane")
    first_core = lax.axis_index("core") == 0
    own_rows = qkv_w.shape[0]
    slots = experts * CAP
    my_shard = lax.axis_index("shard")
    sequence = tokens * shards
    q_heads = HEADS // shards
    kv_heads = KV_HEADS // shards
    group = HEADS // KV_HEADS
    q_width = q_heads * HEAD
    kv_width = kv_heads * HEAD
    own_width = q_width + 2 * kv_width

    width_out = D_MODEL
    out_fold = width_out * own_rows // (shards * own_rows)

    with jax.named_scope("weights_out"):
        extras = jnp.concatenate(
            [router_w, gain_w, jnp.zeros((own_rows, 128 - experts - 2), f32)], axis=1
        ).astype(bf)
        packed = jnp.concatenate(
            [
                split_columns(qkv_w.astype(bf), shards),
                jnp.broadcast_to(extras[:, None], (own_rows, shards, 128)),
            ],
            axis=2,
        )
        moves = [(s * experts + m, m * shards + s) for s in range(shards) for m in range(experts)]
        out_moved = lax.ppermute(out_w.astype(bf), ALL, moves)
        folds = width_out // out_fold
        out_moved = jnp.swapaxes(out_moved.reshape(own_rows, folds, out_fold), 0, 1)
        out_moved = out_moved.reshape(own_rows * folds, out_fold)
        packed = lax.all_to_all(jnp.swapaxes(packed, 0, 1), "shard", 0, 0, tiled=True)
        packed = packed.reshape(shards * own_rows, own_width + 128)
        packed = jnp.concatenate([packed, out_moved], axis=1)
        mine = lax.all_to_all(
            jnp.broadcast_to(packed[None], (planes, *packed.shape)), "plane", 0, 0, tiled=True
        )
    sequence_rows = jnp.concatenate(
        [inputs] + [shift(inputs, shards, k) for k in range(1, shards)], axis=0
    )
    expand_full = lax.all_gather(expand_w.astype(bf), "shard", axis=1, tiled=True)[0]
    reduce_full = lax.all_gather(reduce_w.astype(bf), "shard", axis=1, tiled=True)[0]

    with jax.named_scope("routing"):
        expert_ids = jnp.arange(experts, dtype=jnp.int32)
        chosen = jnp.any(route_ids[:, :, None] == expert_ids[None, None, :], axis=1)
        chosen_b = chosen.astype(bf)
        token_ids = jnp.arange(tokens, dtype=jnp.int32)
        earlier = (token_ids[:, None] > token_ids[None, :]).astype(bf)
        place = jnp.where(chosen, dot(earlier, chosen_b), -1.0).astype(bf)
        slot_ids = jnp.arange(slots, dtype=jnp.int32)
        spread = (slot_ids[None, :] // CAP == expert_ids[:, None]).astype(bf)
        place_of = dot(place, spread)
        select = (place_of == (slot_ids % CAP).astype(f32)[None, :]).astype(bf)

    with jax.named_scope("cotangent_out"):
        grad_sent = dot_tn(select, cotangent).astype(bf).reshape(experts, CAP, D_MODEL)
        grad_sent, mine = after(grad_sent, mine)
        grad_rows = lax.all_to_all(grad_sent, EXPERT, 0, 0, tiled=True).reshape(slots, D_MODEL)

    weights = by_core(first_core, mine, other_core(mine)).reshape(D_MODEL, -1)
    out_own = weights[:, own_width + 128 :].reshape(experts, folds, own_rows, out_fold)
    out_own = jnp.swapaxes(out_own, 1, 2).reshape(q_width, width_out)

    block_ids = (my_shard - jnp.arange(shards, dtype=jnp.int32) + shards) % shards
    positions = (block_ids[:, None] * tokens + token_ids[None, :]).reshape(-1)
    inverse_freq = rope_base ** (-(jnp.arange(HEAD // 2, dtype=f32) * 2.0) / HEAD)
    angles = positions.astype(f32)[:, None] * inverse_freq[None, :]
    cosine = jnp.concatenate([jnp.cos(angles), jnp.cos(angles)], axis=-1)
    sine = jnp.concatenate([jnp.sin(angles), jnp.sin(angles)], axis=-1)
    allowed = positions[:, None] >= positions[None, :]

    with jax.named_scope("attention_in"):
        wide = sequence_rows.astype(f32)
        inverse_one = lax.rsqrt(jnp.mean(wide * wide, axis=-1, keepdims=True) + norm_eps)
        normal_one = wide * inverse_one
        qkv_own = weights[:, :own_width]
        router_full = weights[:, own_width : own_width + experts]
        gains = weights[:, own_width + experts : own_width + experts + 2].astype(f32)
        gain_one = gains[:, 0]
        gain_two = gains[:, 1]
        attend_in = lax.optimization_barrier((normal_one * gain_one).astype(bf))
        qkv = dot(attend_in, qkv_own)
        query = rotary(qkv[:, :q_width].reshape(sequence, q_heads, HEAD), cosine, sine)
        query = query.astype(bf).reshape(sequence, kv_heads, group, HEAD)
        keys = rotary(
            qkv[:, q_width : q_width + kv_width].reshape(sequence, kv_heads, HEAD), cosine, sine
        ).astype(bf)
        values = qkv[:, q_width + kv_width :].astype(bf).reshape(sequence, kv_heads, HEAD)

    with jax.named_scope("attention"):
        scale = HEAD ** (-0.5)
        scores = jnp.einsum("tkgd,skd->kgts", query, keys, preferred_element_type=f32) * scale
        scores = jnp.where(allowed, scores, masked_score)
        row_max = jnp.max(scores, axis=-1, keepdims=True)
        powers = jnp.exp(scores - row_max)
        probs = powers / jnp.sum(powers, axis=-1, keepdims=True)
        probs_b = probs.astype(bf)
        attended_own = jnp.einsum("kgts,skd->tkgd", probs_b, values, preferred_element_type=f32)
        attended_own = attended_own.astype(bf).reshape(sequence, q_width)

    def to_tokens(rows):
        return [rows[:tokens]] + [
            shift(rows[k * tokens : (k + 1) * tokens], shards, -k) for k in range(1, shards)
        ]

    def rotate(blocks):
        start = (shards - my_shard) % shards * q_width
        return lax.dynamic_slice(
            jnp.concatenate([blocks, blocks], axis=1), (0, start), blocks.shape
        )

    def head_block(full, k):
        start = (my_shard + k) % shards * q_width
        return lax.dynamic_slice(full, (0, start), (full.shape[0], q_width))

    def split_rows(grad):
        parts = grad.reshape(planes, 2, grad.shape[0] // experts, -1)
        return (
            jnp.where(first_core, parts[:, 0], parts[:, 1]),
            jnp.where(first_core, parts[:, 1], parts[:, 0]),
        )

    def add_cores(keep, got):
        return (keep.astype(f32) + got.astype(f32)).astype(bf)

    def send_rows(total, axes):
        total = total.reshape(-1, own_rows, total.shape[-1])
        return lax.all_to_all(total, axes, 0, 0, tiled=True)

    with jax.named_scope("attention_out"):
        branch_part = dot(attended_own, out_own)
        pieces = to_tokens(branch_part.astype(bf))
        branch = branch_part[:tokens] + sum(piece.astype(f32) for piece in pieces[1:])
        state = inputs.astype(f32) + branch
        inverse_two = lax.rsqrt(jnp.mean(state * state, axis=-1, keepdims=True) + norm_eps)
        normal_two = state * inverse_two
        mixed_in = (normal_two * gain_two).astype(bf)

    with jax.named_scope("gates"):
        logits = jnp.where(chosen, dot(mixed_in, router_full), masked_score)
        top_logit = jnp.max(logits, axis=-1, keepdims=True)
        gate_power = jnp.where(chosen, jnp.exp(logits - top_logit), 0.0)
        gates = gate_power / jnp.sum(gate_power, axis=-1, keepdims=True)
        gate_spread = jnp.dot(gates, spread.astype(f32), precision=HIGHEST)
        gate_select = gate_spread * select.astype(f32)
        gates_high = gates.astype(bf)
        gates_low = (gates - gates_high.astype(f32)).astype(bf)
        gate_lanes = jnp.concatenate(
            [gates_high, gates_low, jnp.zeros((tokens, 128 - 2 * experts), bf)], axis=1
        )

    with jax.named_scope("dispatch"):
        sent = dot_tn(select, jnp.concatenate([mixed_in, gate_lanes], axis=1)).astype(bf)
        sent = sent.reshape(experts, CAP, D_MODEL + 128)
        sent, grad_rows = after(sent, grad_rows)
        attended_sent, sent = after(attended_own, sent)
        attended = rotate(jnp.concatenate(to_tokens(attended_sent), axis=1))
        out_full = lax.all_gather(out_own, "shard", axis=0, tiled=True)
        arrived = lax.all_to_all(sent, EXPERT, 0, 0, tiled=True).reshape(slots, D_MODEL + 128)
        lane = jnp.arange(128, dtype=jnp.int32)
        mine = (lane < 2 * experts) & (lane % experts == lax.axis_index(EXPERT))
        gate_rows = jnp.sum(
            jnp.where(mine, arrived[:, D_MODEL:].astype(f32), 0.0), axis=1, keepdims=True
        )

    with jax.named_scope("experts"):
        expand_padded = jnp.pad(expand_full, ((0, 128), (0, 0)))
        gate_part = dot(arrived, expand_padded[:, :FF])
        up_part = dot(arrived, expand_padded[:, FF:])
        hidden = (gate_part * jax.nn.sigmoid(gate_part) * up_part).astype(bf)
        produced = dot(hidden, reduce_full).astype(bf)
        returned = lax.all_to_all(
            produced.reshape(experts, CAP, D_MODEL), EXPERT, 0, 0, tiled=True
        ).reshape(slots, D_MODEL)
        grad_rows, gate_rows, arrived, hidden, produced = after(
            grad_rows, gate_rows, arrived, hidden, produced
        )
        hidden_grad = dot_nt(grad_rows, reduce_full)
        gate_up = dot(arrived, expand_padded)
        gate_part = gate_up[:, :FF]
        up_part = gate_up[:, FF:]
        sigmoid_gate = jax.nn.sigmoid(gate_part)
        silu_gate = gate_part * sigmoid_gate
        hidden_gated = (hidden.astype(f32) * gate_rows).astype(bf)
        hidden_grad = hidden_grad * gate_rows
        gate_side = hidden_grad * up_part * sigmoid_gate * (1.0 + gate_part * (1.0 - sigmoid_gate))
        up_side = hidden_grad * silu_gate
        gate_up_grad = jnp.concatenate([gate_side, up_side], axis=1).astype(bf)
        row_grad = dot_nt(gate_up_grad, expand_full).astype(bf).reshape(experts, CAP, D_MODEL)
        row_grad, returned, out_full = after(row_grad, returned, out_full)
        hidden_gated, arrived, returned = after(hidden_gated, arrived, returned)
        rows_back = lax.all_to_all(row_grad, EXPERT, 0, 0, tiled=True).reshape(slots, D_MODEL)
        reduce_grad = dot_tn(hidden_gated, grad_rows)
        expand_grad = dot_tn(arrived, gate_up_grad)[:D_MODEL].astype(bf)
        reduce_sum = lax.psum_scatter(
            reduce_grad[None].astype(bf), "shard", scatter_dimension=1, tiled=True
        )

    with jax.named_scope("outputs"):
        gate_high = gate_select.astype(bf)
        gate_low = (gate_select - gate_high.astype(f32)).astype(bf)
        outputs = (state + (dot(gate_high, returned) + dot(gate_low, returned))).astype(bf)
        rows_back, outputs, expand_grad = after(rows_back, outputs, expand_grad)
        expand_sum = lax.psum_scatter(
            expand_grad[None], "shard", scatter_dimension=1, tiled=True
        )

    with jax.named_scope("state_grad"):
        pair_dots = dot_nt(cotangent, returned) * select.astype(f32)
        gate_grad = jnp.dot(pair_dots, spread.astype(f32).T, precision=HIGHEST)
        mean_gate = jnp.sum(gates * gate_grad, axis=-1, keepdims=True)
        logit_grad = (gates * (gate_grad - mean_gate)).astype(bf)
        grad_out = cotangent.astype(f32)
        mixed_grad = dot(select, rows_back) + dot_nt(logit_grad, router_full)
        scaled_two = mixed_grad * gain_two
        gain_two_grad = jnp.sum(mixed_grad * normal_two, axis=0)
        state_grad = grad_out + inverse_two * (
            scaled_two - normal_two * jnp.mean(scaled_two * normal_two, axis=-1, keepdims=True)
        )
        branch_grad = state_grad.astype(bf)

    with jax.named_scope("out_grad"):
        out_keep, out_give = split_rows(dot_tn(attended, branch_grad).astype(bf))
        branch_grad, out_give = after(branch_grad, out_give)
        attended_grad = dot_nt(branch_grad, out_full).astype(bf)
        attended_grad_own = jnp.concatenate(
            [head_block(attended_grad, 0)]
            + [shift(head_block(attended_grad, k), shards, k) for k in range(1, shards)],
            axis=0,
        ).reshape(sequence, kv_heads, group, HEAD)
        out_total = add_cores(out_keep, other_core(out_give))
        attended_grad_own, out_total = after(attended_grad_own, out_total)
        out_parts = send_rows(out_total, CHIPS)
        out_sum = jnp.sum(out_parts.astype(f32), axis=0)

    with jax.named_scope("attention_grad"):
        prob_grad = jnp.einsum(
            "tkgd,skd->kgts", attended_grad_own, values, preferred_element_type=f32
        )
        row_dot = jnp.sum(probs * prob_grad, axis=-1, keepdims=True)
        score_grad = (probs * (prob_grad - row_dot)).astype(bf)
        query_grad = (
            jnp.einsum("kgts,skd->tkgd", score_grad, keys, preferred_element_type=f32) * scale
        )
        key_grad = (
            jnp.einsum("kgts,tkgd->skd", score_grad, query, preferred_element_type=f32) * scale
        )
        value_grad = jnp.einsum(
            "kgts,tkgd->skd", probs_b, attended_grad_own, preferred_element_type=f32
        )
        query_back = rotary_back(
            query_grad.reshape(sequence, q_heads, HEAD), cosine, sine
        ).reshape(sequence, q_width)
        key_back = rotary_back(key_grad, cosine, sine).reshape(sequence, kv_width)
        qkv_grad = jnp.concatenate(
            [query_back, key_back, value_grad.reshape(sequence, kv_width)], axis=1
        ).astype(bf)

    with jax.named_scope("qkv_grad"):
        extras_grad = jnp.concatenate(
            [
                dot_tn(mixed_in, logit_grad),
                gain_two_grad[:, None],
                jnp.zeros((D_MODEL, 127 - experts), f32),
            ],
            axis=1,
        ).astype(bf)
        qkv_sent = jnp.concatenate(
            [dot_tn(attend_in, qkv_grad).astype(bf), extras_grad], axis=1
        )
        qkv_keep, qkv_give = split_rows(qkv_sent)
        qkv_grad, qkv_give = after(qkv_grad, qkv_give)
        attend_grad_part = dot_nt(qkv_grad, qkv_own)
        qkv_give, attend_grad_sent, out_parts = after(
            qkv_give, attend_grad_part.astype(bf), out_parts
        )
        qkv_part = add_cores(qkv_keep, other_core(qkv_give))
        attend_grad_sent, expand_sum, reduce_sum, qkv_part = after(
            attend_grad_sent, expand_sum, reduce_sum, qkv_part
        )
        qkv_parts = send_rows(qkv_part, CHIPS)
        qkv_total = jnp.sum(
            qkv_parts.reshape(planes, shards, own_rows, own_width + 128).astype(f32), axis=0
        )
        qkv_sum = join_columns(qkv_total[:, :, :own_width], shards)
        extras_sum = jnp.sum(qkv_total[:, :, own_width:], axis=0)
        router_sum = extras_sum[:, :experts]
        gain_two_sum = extras_sum[:, experts : experts + 1]
        gain_one_sum = jnp.sum(
            qkv_w.astype(bf).astype(f32) * qkv_sum, axis=1, keepdims=True
        ) / gain_w[:, :1].astype(bf).astype(f32)
        gain_sum = jnp.concatenate([gain_one_sum, gain_two_sum], axis=1)

    with jax.named_scope("input_grad"):
        attend_pieces = to_tokens(attend_grad_sent)
        attend_grad = sum(piece.astype(f32) for piece in attend_pieces)
        own_normal = normal_one[:tokens]
        scaled_one = attend_grad * gain_one
        input_grad = state_grad + inverse_one[:tokens] * (
            scaled_one - own_normal * jnp.mean(scaled_one * own_normal, axis=-1, keepdims=True)
        )

    with jax.named_scope("update"):
        qkv_new = adamw(qkv_w, qkv_sum, qkv_m, qkv_v, rate_inputs, matrix_decay)
        out_new = adamw(out_w, out_sum, out_m, out_v, rate_output, matrix_decay)
        router_new = adamw(router_w, router_sum, router_m, router_v, rate_router, matrix_decay)
        gain_new = adamw(gain_w, gain_sum, gain_m, gain_v, rate_gains, 0.0)
        expand_new = adamw(expand_w, expand_sum.astype(f32), expand_m, expand_v, rate_expand, matrix_decay)
        reduce_new = adamw(reduce_w, reduce_sum.astype(f32), reduce_m, reduce_v, rate_reduce, matrix_decay)
    return (
        outputs,
        input_grad,
        *qkv_new,
        *out_new,
        *router_new,
        *gain_new,
        *expand_new,
        *reduce_new,
    )


def solution(mesh):
    experts, shards = mesh.shape["expert"], mesh.shape["shard"]
    split = Mesh(mesh.devices.reshape(experts // 2, 2, shards), ("plane", "core", "shard"))
    rows = P(("plane", "core", "shard"), None)
    expert = P(EXPERT, "shard", None)
    return jax.shard_map(
        local,
        mesh=split,
        in_specs=(rows,) * 15 + (expert,) * 6,
        out_specs=(rows,) * 14 + (expert,) * 6,
        check_vma=False,
    )
```
